32 devices in a mesh: exp: 8 (over z, x), tp: 4 (over y, core).
Axes of the slice: x: 2, y: 2, z: 4, core: 2. Of those that a mesh axis runs over, the one named last changes fastest.
Arguments:
- tokens: bfloat16 [24576, 768], P(('exp', 'tp')), may hold values from -6 to 6
- segments: int32 [48, 512], P('exp'), may hold values from 0 to 3, never falling along the last dimension, each value on 1 to 256 neighbouring positions
- routes: int32 [24576], P(('exp', 'tp')), may hold values from 0 to 7, as said below
- attn_gain: float32 [768], replicated, may hold values from 0.1 to 1.9
- w_query: bfloat16 [768, 768], P(None, 'tp'), may hold values from -0.0546875 to 0.0546875
- w_key: bfloat16 [768, 768], P(None, 'tp'), may hold values from -0.21875 to 0.21875
- w_value: bfloat16 [768, 768], P(None, 'tp'), may hold values from -0.21875 to 0.21875
- w_output: bfloat16 [768, 768], P('tp'), may hold values from -1.25 to 1.25
- bias_table: float32 [32, 12], P(None, 'tp'), may hold values from -4 to 4
- ffn_gain: float32 [768], replicated, may hold values from 0.1 to 1.9
- w_router: bfloat16 [768, 8], replicated, may hold values from -0.15625 to 0.15625
- expert_in: bfloat16 [8, 768, 3072], P('exp', None, 'tp'), may hold values from -0.21875 to 0.21875
- expert_out: bfloat16 [8, 3072, 768], P('exp', 'tp'), as said below
- cotangent: bfloat16 [24576, 768], P(('exp', 'tp')), may hold values from -6 to 6
Outputs:
- mixed: bfloat16 [24576, 768], P(('exp', 'tp'))
- grad_tokens: float32 [24576, 768], P(('exp', 'tp'))
- grad_attn_gain: float32 [768], replicated
- grad_w_query: float32 [768, 768], P(None, 'tp')
- grad_w_key: float32 [768, 768], P(None, 'tp')
- grad_w_value: float32 [768, 768], P(None, 'tp')
- grad_w_output: float32 [768, 768], P('tp')
- grad_bias_table: float32 [32, 12], P(None, 'tp')
- grad_ffn_gain: float32 [768], replicated
- grad_w_router: float32 [768, 8], replicated
- grad_expert_in: float32 [8, 768, 3072], P('exp', None, 'tp')
- grad_expert_out: float32 [8, 3072, 768], P('exp', 'tp')
The draws below stay inside these ranges and needn't reach their ends.
Inputs may be any that keep to these rules, and one draw needn't show every extreme that they name: `routes`: each token's expert. In every aligned block of 768 tokens one expert, the same for all blocks, is named by 120 + 24 tokens, and every other expert by at most 120. `segments`: document numbers within each sequence, never falling along it. `expert_out`: expert output weights, normal with width 1.5 × 8 / sqrt(3072) and clipped at 4 widths, so they grow with the number of experts: ±0.8671875 with 8 experts, ±6.9375 with 64.
All inputs are finite; a program needn't handle non-finite values.
Results may differ from the reference program's by a relative error of at most 0.017.
The reference program's roundings to bfloat16 on the way count: a program that leaves them out, or rounds other values in their place, can miss the bound.
Values may be sent and summed in bfloat16 or wider, within the bound.
No kernel may reach another device: no remote copies, remote signals or barrier semaphores. Data moves between devices by JAX's collectives and lax.ppermute only.
A program may use at most 256 MiB of HBM per device.

```python
import math
import jax
import jax.numpy as jnp
import numpy as np
from jax import lax

D = 768
HEADS = 12
HEAD_DIM = 64
FF = 3072
BUCKETS = 32
SEQ_LEN = 512
EXPERTS = 8
ROWS = 768
SEQUENCES = 48
TOKENS = 24576
CAP_SRC = 120
DROPS = 24


def draw_routes(key, part):
    key = jax.random.fold_in(key, 11)
    blocks = TOKENS // ROWS
    slots = EXPERTS * CAP_SRC
    favored = jax.random.randint(jax.random.fold_in(key, 1), (), 0, EXPERTS).astype(jnp.int32)
    loads = jax.random.randint(jax.random.fold_in(key, 2), (EXPERTS,), 1, 5).astype(jnp.int32)
    owner = jnp.arange(slots, dtype=jnp.int32) // CAP_SRC

    def one_block(block_key):
        score_key, order_key = jax.random.split(block_key)
        base_score = jax.random.randint(score_key, (slots,), 0, 65536).astype(jnp.int32) * loads[owner]
        score = jnp.where(owner == favored, 4 * 65536, base_score) * slots + jnp.arange(slots, dtype=jnp.int32)
        chosen = owner[jnp.argsort(-score)[:ROWS - DROPS]]
        chosen = jnp.concatenate([chosen, jnp.full((DROPS,), favored, jnp.int32)])
        return chosen[jax.random.permutation(order_key, ROWS)]
    block_keys = jax.random.split(jax.random.fold_in(key, 3), blocks)
    return jax.vmap(one_block)(block_keys).reshape(TOKENS).astype(jnp.int32)


def draw_expert_out(key, part):
    key = jax.random.fold_in(key, 7)
    values = jnp.clip(jax.random.normal(key, (EXPERTS, FF, D), jnp.float32), -4.0, 4.0)
    return (values * (1.5 * EXPERTS / math.sqrt(FF))).astype(jnp.bfloat16)


def levels(rng, dims, cuts, least, high):
    def one(axis_at, blocks):
        heights = jax.random.uniform(jax.random.fold_in(jax.random.fold_in(rng, 6), axis_at), (blocks,), jnp.float32, least / len(cuts), high / len(cuts))
        return jnp.repeat(jnp.exp(heights), dims[axis_at] // blocks).reshape((-1,) + (1,) * (len(dims) - axis_at - 1))

    level = one(*cuts[0])
    for cut in cuts[1:]:
        level = level * one(*cut)
    return level


def length_profile(number_of, total, most, slope):
    weights = [(1 << 20) // math.isqrt(grade ** slope) + 1 for grade in range(2, number_of + 1)]
    rest, holding = total - most - (number_of - 1), [1] * (number_of - 1)
    while rest > 0:
        movable = [i for i in range(number_of - 1) if holding[i] < most]
        mass, left = sum([weights[i] for i in movable]), rest
        for i in movable:
            addition = min(most - holding[i], max(1, left * weights[i] // mass), rest)
            holding[i] = holding[i] + addition
            rest = rest - addition
    return np.array([most] + holding)


def ragged_sizes(key, number_of, total, limit, slope):
    if number_of == 2:
        one = jax.random.randint(key, (), max(1, total - limit), min(limit, total - 1) + 1)
        return jnp.stack([one, total - one])
    lengths = jnp.asarray(length_profile(number_of, total, limit, slope), jnp.int32)
    twos = (number_of - 1) // 2
    giver, taker = lengths[1:1 + 2 * twos:2], lengths[2:2 + 2 * twos:2]
    room = jnp.minimum(giver - 1, limit - taker)
    shifted = jax.random.randint(jax.random.fold_in(key, 1), (twos,), 0, 1 << 20) % (room + 1)
    lengths = lengths.at[1:1 + 2 * twos:2].set(giver - shifted).at[2:2 + 2 * twos:2].set(taker + shifted)
    return lengths[jax.random.permutation(jax.random.fold_in(key, 2), number_of)]


def normal_values(own_key, shape, width, bound, cuts=(), held_as=jnp.bfloat16):
    result = jax.random.normal(own_key, shape, jnp.float32) * width
    if len(cuts) > 0:
        result = levels(own_key, shape, cuts, -0.22, 0.18) * result
    return jnp.clip(result, min=-bound, max=bound).astype(held_as)


def setup_inputs(seed: int = 0) -> dict:
    splits = jax.random.split(jax.random.key(seed), 15)
    return {
        "tokens": normal_values(splits[0], (TOKENS, D), 1.0, 6.0, ((0, 32),)),
        "segments": jax.vmap(lambda own: jnp.searchsorted(jnp.cumsum(ragged_sizes(own, 4, SEQ_LEN, SEQ_LEN // 2, 1)), jnp.arange(SEQ_LEN), side="right"))(jax.random.split(splits[1], SEQUENCES)).reshape((SEQUENCES, SEQ_LEN)).astype(jnp.int32),
        "routes": draw_routes(jax.random.fold_in(splits[14], 71), 0),
        "attn_gain": jnp.clip(1.0 + 0.18 * jax.random.normal(splits[3], (D,), jnp.float32), 0.1, 1.9),
        "w_query": normal_values(splits[4], (D, HEADS * HEAD_DIM), (16 * D) ** -0.5, 0.0546875, ((1, 4),)),
        "w_key": normal_values(splits[5], (D, HEADS * HEAD_DIM), D ** -0.5, 0.21875, ((1, 4),)),
        "w_value": normal_values(splits[6], (D, HEADS * HEAD_DIM), D ** -0.5, 0.21875, ((1, 4),)),
        "w_output": normal_values(splits[7], (HEADS * HEAD_DIM, D), (max(HEADS * HEAD_DIM // 32, 8)) ** -0.5, 1.25, ((0, 4),)),
        "bias_table": normal_values(splits[8], (BUCKETS, HEADS), 1.0, 4.0, ((1, 4),), jnp.float32),
        "ffn_gain": jnp.clip(1.0 + 0.18 * jax.random.normal(splits[9], (D,), jnp.float32), 0.1, 1.9),
        "w_router": normal_values(splits[10], (D, EXPERTS), (2 * D) ** -0.5, 0.15625),
        "expert_in": normal_values(splits[11], (EXPERTS, D, FF), D ** -0.5, 0.21875, ((0, 8), (2, 4))),
        "expert_out": draw_expert_out(jax.random.fold_in(splits[14], 71), 0),
        "cotangent": normal_values(splits[13], (TOKENS, D), 1.0, 6.0, ((0, 32),)),
    }


EPSILON = 1e-06
MASKED_SCORE = -1000000000.0
thresholds = (8, 12, 16, 23, 32, 46, 64, 91)

@jax.custom_vjp
def low(v):
    return lax.optimization_barrier(v.astype(jnp.bfloat16)).astype(jnp.float32)

@jax.custom_vjp
def low_back(v):
    return v

def low_keep(v):
    return (low(v), None)

def low_pass(kept, grad):
    return (grad,)

def back_keep(v):
    return (v, None)

def back_low(kept, grad):
    return (low(grad),)
low.defvjp(low_keep, low_pass)
low_back.defvjp(back_keep, back_low)

def bucket_rows(length, first, count):
    query_place = first + jnp.arange(count, dtype=jnp.int32)
    key_place = jnp.arange(length, dtype=jnp.int32)
    relative = key_place[None, :] - query_place[:, None]
    distance = jnp.abs(relative)
    distant = 7 + sum(((distance >= boundary).astype(jnp.int32) for boundary in thresholds))
    return jnp.where(distance < 8, distance, distant) + jnp.where(relative > 0, 16, 0)

def rms_apply(values, gain):
    scale = lax.rsqrt(lax.optimization_barrier(jnp.mean(values * values, axis=-1, keepdims=True)) + EPSILON)
    return values * scale * gain

def highest(left, right):
    return jnp.dot(left, right, precision=lax.Precision.HIGHEST, preferred_element_type=jnp.float32)

def reference(tokens, segments, routes, attn_gain, w_query, w_key, w_value, w_output, bias_table, ffn_gain, w_router, expert_in, expert_out, cotangent):
    blocks = TOKENS // ROWS
    slots = EXPERTS * blocks * CAP_SRC
    choose = (routes[:, None] == jnp.arange(EXPERTS, dtype=jnp.int32)[None, :]).astype(jnp.int32)
    grouped = choose.reshape(blocks, ROWS, EXPERTS)
    rank = jnp.cumsum(grouped, axis=1) - grouped
    slot = lax.optimization_barrier(jnp.sum(rank * grouped, axis=-1)).reshape(TOKENS)
    source = jnp.arange(TOKENS, dtype=jnp.int32) // ROWS
    target = jnp.where(slot < CAP_SRC, routes * (blocks * CAP_SRC) + source * CAP_SRC + slot, slots).astype(jnp.int32)
    choose_float = choose.astype(jnp.float32)
    buckets = bucket_rows(SEQ_LEN, 0, SEQ_LEN)
    group = math.gcd(SEQUENCES, max(1, 4096 // SEQ_LEN))

    def grouped_view(array):
        return array.reshape((SEQUENCES // group, group) + array.shape[1:])

    def forward(inputs, gain_one, query_w, key_w, value_w, output_w, table, gain_two, router_w, in_w, out_w):
        normed = low(rms_apply(inputs, gain_one))
        query = low_back(low(highest(normed, query_w))).reshape(SEQUENCES, SEQ_LEN, HEADS, HEAD_DIM)
        key = low_back(low(highest(normed, key_w))).reshape(SEQUENCES, SEQ_LEN, HEADS, HEAD_DIM)
        value = low_back(low(highest(normed, value_w))).reshape(SEQUENCES, SEQ_LEN, HEADS, HEAD_DIM)
        bias = jnp.transpose(jnp.take(table, buckets, axis=0), (2, 0, 1))

        def attend(block):
            block_query, block_key, block_value, block_segments = block
            scores = jnp.einsum('gqhd,gkhd->ghqk', block_query, block_key, precision=lax.Precision.HIGHEST) + bias[None]
            scores = low_back(scores)
            same = (block_segments[:, :, None] == block_segments[:, None, :])[:, None]
            weights = low(jax.nn.softmax(jnp.where(same, scores, MASKED_SCORE), axis=-1))
            return jnp.einsum('ghqk,gkhd->gqhd', weights, block_value, precision=lax.Precision.HIGHEST)
        heads = lax.map(jax.checkpoint(attend), (grouped_view(query), grouped_view(key), grouped_view(value), grouped_view(segments)))
        attended = low_back(low(heads.reshape(TOKENS, HEADS * HEAD_DIM)))
        residual = inputs + low_back(highest(attended, output_w))
        mixed_in = low(rms_apply(residual, gain_two))
        router_share = jax.nn.softmax(low_back(highest(mixed_in, router_w)), axis=-1)
        gate = lax.optimization_barrier(jnp.sum(router_share * choose_float, axis=-1))
        buffer = jnp.zeros((slots + 1, D), jnp.float32).at[target].set(mixed_in)[:slots]
        buffer = low_back(buffer).reshape(EXPERTS, blocks * CAP_SRC, D)

        def expert(item):
            rows, weight_in, weight_out = item
            upper = low_back(highest(rows, weight_in))
            active = low(jax.nn.gelu(upper))
            return low_back(low(highest(active, weight_out)))
        produced = lax.map(jax.checkpoint(expert), (buffer, in_w, out_w))
        padded = jnp.concatenate([produced.reshape(slots, D), jnp.zeros((1, D), jnp.float32)], axis=0)
        returned = jnp.take(padded, target, axis=0)
        return residual + gate[:, None] * returned
    mixed, pullback = jax.vjp(forward, tokens.astype(jnp.float32), attn_gain.astype(jnp.float32), w_query.astype(jnp.float32), w_key.astype(jnp.float32), w_value.astype(jnp.float32), w_output.astype(jnp.float32), bias_table.astype(jnp.float32), ffn_gain.astype(jnp.float32), w_router.astype(jnp.float32), expert_in.astype(jnp.float32), expert_out.astype(jnp.float32))
    grads = pullback(cotangent.astype(jnp.float32))
    return (mixed.astype(jnp.bfloat16), grads[0], grads[1], grads[2], grads[3], grads[4], grads[5], grads[6], grads[7], grads[8], grads[9], grads[10])
```

```python
import functools

import jax
import jax.numpy as jnp
from jax import lax
from jax.sharding import PartitionSpec as P

HEAD_DIM = 64


EPSILON = 1e-06
MASKED_SCORE = -1000000000.0
thresholds = (8, 12, 16, 23, 32, 46, 64, 91)


def bucket_rows(length, first, count):
    query_place = first + jnp.arange(count, dtype=jnp.int32)
    key_place = jnp.arange(length, dtype=jnp.int32)
    relative = key_place[None, :] - query_place[:, None]
    distance = jnp.abs(relative)
    distant = 7 + sum(((distance >= boundary).astype(jnp.int32) for boundary in thresholds))
    return jnp.where(distance < 8, distance, distant) + jnp.where(relative > 0, 16, 0)


def rms_scale(values):
    return lax.rsqrt(jnp.mean(values * values, axis=-1, keepdims=True) + EPSILON)


def rms_apply(values, gain):
    return values * rms_scale(values) * gain


def bucket_onehot(length, first, count, table_rows):
    buckets = bucket_rows(length, first, count)
    return (buckets[:, :, None] == jnp.arange(table_rows, dtype=jnp.int32)[None, None, :]).astype(
        jnp.float32
    )


def position_bias(table, length):
    block = min(length, 128)
    pieces = []
    for first in range(0, length, block):
        onehot = bucket_onehot(length, first, block, table.shape[0])
        pieces.append(jnp.einsum("qkb,bh->hqk", onehot, table, precision=lax.Precision.HIGHEST))
    return jnp.concatenate(pieces, axis=1)


def table_grad(score_total, table_rows, length):
    block = min(length, 128)
    total = jnp.zeros((table_rows, score_total.shape[0]), jnp.float32)
    for first in range(0, length, block):
        onehot = bucket_onehot(length, first, block, table_rows)
        total = total + jnp.einsum(
            "qkb,hqk->bh",
            onehot,
            score_total[:, first : first + block],
            precision=lax.Precision.HIGHEST,
        )
    return total


def dot(left, right):
    return jnp.dot(left, right, preferred_element_type=jnp.float32)


def contract_first(left, right):
    return lax.dot_general(
        left, right, (((0,), (0,)), ((), ())), preferred_element_type=jnp.float32
    )


def contract_last(left, right):
    return lax.dot_general(
        left, right, (((1,), (1,)), ((), ())), preferred_element_type=jnp.float32
    )


def gelu_both(upper):
    slope = 0.7978845608028654
    square = upper * upper
    bend = jnp.tanh(slope * upper * (1.0 + 0.044715 * square))
    half = 0.5 * (1.0 + bend)
    active = upper * half
    derivative = half + 0.5 * upper * (1.0 - bend * bend) * slope * (1.0 + 3 * 0.044715 * square)
    return active, derivative


def swap(value, axis, size, bit):
    return lax.ppermute(value, axis, [(place, place ^ bit) for place in range(size)])


def exchange(blocks, axis, size):
    stride = 1
    while stride < size:
        digit = min(8, size // stride)
        shape = blocks.shape
        view = blocks.reshape((size // (stride * digit), digit, stride) + shape[1:])
        parts = [view[:, 0]]
        for step in range(1, digit):
            parts.append(swap(view[:, step], axis, size, step * stride))
        blocks = jnp.stack(parts, axis=1).reshape(shape)
        stride *= digit
    return blocks


def shared_sum(value, axis, size):
    bit = 1
    while bit < size:
        value = value + swap(value, axis, size, bit)
        bit *= 2
    return value


def wide_sum(value, axis, size, bits):
    me = lax.axis_index(axis)
    for bit in bits:
        half = value.shape[0] // 2
        side = (me // bit) % 2
        keep = lax.dynamic_slice_in_dim(value, side * half, half, 0)
        send = lax.dynamic_slice_in_dim(value, (1 - side) * half, half, 0)
        value = keep + swap(send.astype(jnp.bfloat16), axis, size, bit).astype(jnp.float32)
    value = value.astype(jnp.bfloat16)
    for bit in reversed(bits):
        other = swap(value, axis, size, bit)
        value = jnp.where(
            (me // bit) % 2 == 0,
            jnp.concatenate([value, other], axis=0),
            jnp.concatenate([other, value], axis=0),
        )
    return value.astype(jnp.float32)


def attend(whole, segments, w_joint, bias):
    seq_count, length = segments.shape
    head_width = w_joint.shape[1] // 3
    heads = head_width // HEAD_DIM
    joint = dot(whole, w_joint).astype(jnp.bfloat16)
    shaped = joint.reshape(seq_count, length, 3, heads, HEAD_DIM)
    same = segments[:, :, None] == segments[:, None, :]
    outputs = []
    log_totals = []
    for index in range(seq_count):
        scores = (
            jnp.einsum(
                "qhd,khd->hqk",
                shaped[index, :, 0],
                shaped[index, :, 1],
                preferred_element_type=jnp.float32,
            )
            + bias
        )
        masked = jnp.where(same[index][None], scores, MASKED_SCORE)
        peak = jnp.max(masked, axis=-1, keepdims=True)
        unscaled = jnp.exp(masked - peak)
        total = jnp.sum(unscaled, axis=-1, keepdims=True)
        log_totals.append(peak + jnp.log(total))
        weight_low = (unscaled / total).astype(jnp.bfloat16)
        heads_out = jnp.einsum(
            "hqk,khd->qhd", weight_low, shaped[index, :, 2], preferred_element_type=jnp.float32
        )
        outputs.append(heads_out.reshape(length, head_width))
    attended = jnp.concatenate(outputs, axis=0).astype(jnp.bfloat16)
    return attended, (shaped, same, log_totals)


def attend_back(kept, whole, attended, grad_whole, w_joint, w_out, bias):
    shaped, same, log_totals = kept
    seq_count, length, _, heads, _ = shaped.shape
    head_width = heads * HEAD_DIM
    grad_w_out = contract_first(attended, grad_whole)
    grad_heads = (
        contract_last(grad_whole, w_out)
        .astype(jnp.bfloat16)
        .reshape(seq_count, length, heads, HEAD_DIM)
    )
    score_total = jnp.zeros((heads, length, length), jnp.float32)
    joint_grads = []
    for index in range(seq_count):
        query = shaped[index, :, 0]
        key = shaped[index, :, 1]
        value = shaped[index, :, 2]
        grad_head = grad_heads[index]
        scores = jnp.einsum("qhd,khd->hqk", query, key, preferred_element_type=jnp.float32) + bias
        masked = jnp.where(same[index][None], scores, MASKED_SCORE)
        weight_full = jnp.exp(masked - log_totals[index])
        weight_low = weight_full.astype(jnp.bfloat16)
        grad_value = jnp.einsum(
            "hqk,qhd->khd", weight_low, grad_head, preferred_element_type=jnp.float32
        )
        grad_weight = jnp.einsum(
            "qhd,khd->hqk", grad_head, value, preferred_element_type=jnp.float32
        )
        delta = jnp.sum(weight_full * grad_weight, axis=-1, keepdims=True)
        grad_scores = (weight_full * (grad_weight - delta)).astype(jnp.bfloat16)
        grad_query = jnp.einsum(
            "hqk,khd->qhd", grad_scores, key, preferred_element_type=jnp.float32
        )
        grad_key = jnp.einsum(
            "hqk,qhd->khd", grad_scores, query, preferred_element_type=jnp.float32
        )
        score_total = score_total + grad_scores.astype(jnp.float32)
        joint_grads.append(
            jnp.stack([grad_query, grad_key, grad_value], axis=1).reshape(length, 3 * head_width)
        )
    grad_joint = jnp.concatenate(joint_grads, axis=0).astype(jnp.bfloat16)
    grad_w_joint = contract_first(whole, grad_joint)
    grad_normed = contract_last(grad_joint, w_joint)
    return grad_w_joint, grad_w_out, score_total, grad_normed


def local(
    sizes,
    tokens,
    segments,
    routes,
    attn_gain,
    w_query,
    w_key,
    w_value,
    w_output,
    bias_table,
    ffn_gain,
    w_router,
    expert_in,
    expert_out,
    cotangent,
):
    n_exp, n_tp = sizes
    rows, width = tokens.shape
    group_seqs, length = segments.shape
    head_width = w_query.shape[1]
    experts = w_router.shape[1]
    capacity = rows * 5 // (4 * experts)
    low = jnp.bfloat16
    my_exp = lax.axis_index("exp")
    my_tp = lax.axis_index("tp")
    my_core = my_tp % 2
    pair_seqs = group_seqs * 2 // n_tp
    seqs = lax.dynamic_slice_in_dim(segments, (my_tp // 2) * pair_seqs, pair_seqs, 0)

    def both(mine, other):
        return jnp.where(
            my_core == 0,
            jnp.concatenate([mine, other], axis=0),
            jnp.concatenate([other, mine], axis=0),
        )

    def mine_of(pair):
        return lax.dynamic_slice_in_dim(pair, my_core * rows, rows, 0)

    def other_of(pair):
        return lax.dynamic_slice_in_dim(pair, (1 - my_core) * rows, rows, 0)

    w_joint = jnp.concatenate([w_query, w_key, w_value], axis=1)
    w_joint_far = swap(w_joint, "tp", n_tp, 2)
    w_output_far = swap(w_output, "tp", n_tp, 2)
    table_far = swap(bias_table, "tp", n_tp, 2)

    place = jnp.arange(rows, dtype=jnp.int32)
    choose = routes[:, None] == jnp.arange(experts, dtype=jnp.int32)[None, :]
    choose_float = choose.astype(jnp.float32)
    rank = dot((place[:, None] > place[None, :]).astype(low), choose.astype(low))
    slot = jnp.sum(rank * choose_float, axis=-1).astype(jnp.int32)
    target = jnp.where(slot < capacity, (routes ^ my_exp) * capacity + slot, experts * capacity)
    spread = (
        target[None, :] == jnp.arange(experts * capacity, dtype=jnp.int32)[:, None]
    ).astype(low)

    def pack(data):
        return dot(spread, data).astype(low).reshape(experts, capacity, width)

    def unpack(data):
        return contract_first(spread, data)

    cotangent_sent = exchange(pack(cotangent), "exp", n_exp)

    inputs = tokens.astype(jnp.float32)
    scale_one = rms_scale(inputs)
    normed_low = (inputs * scale_one * attn_gain).astype(low)
    whole = both(normed_low, swap(normed_low, "tp", n_tp, 1))
    bias = position_bias(bias_table, length)
    bias_far = position_bias(table_far, length)
    attended, kept = attend(whole, seqs, w_joint, bias)

    expert_in_far = swap(expert_in[0], "tp", n_tp, 2)
    expert_out_far = swap(expert_out[0], "tp", n_tp, 2)
    ins = [expert_in[0], swap(expert_in[0], "tp", n_tp, 1)]
    ins += [expert_in_far, swap(expert_in_far, "tp", n_tp, 1)]
    outs = [expert_out[0], swap(expert_out[0], "tp", n_tp, 1)]
    outs += [expert_out_far, swap(expert_out_far, "tp", n_tp, 1)]

    attended_far, kept_far = attend(whole, seqs, w_joint_far, bias_far)
    partial = dot(attended, w_output) + dot(attended_far, w_output_far)
    residual = inputs + (mine_of(partial) + swap(other_of(partial), "tp", n_tp, 1))

    scale_two = rms_scale(residual)
    mixed_low = (residual * scale_two * ffn_gain).astype(low)
    router_share = jax.nn.softmax(dot(mixed_low, w_router), axis=-1)
    gate = jnp.sum(router_share * choose_float, axis=-1)
    received = exchange(pack(mixed_low), "exp", n_exp).reshape(-1, width)

    cotangent_rows = cotangent_sent.reshape(-1, width).astype(jnp.float32)
    share_rows = jax.nn.softmax(dot(received, w_router), axis=-1)
    is_mine = (jnp.arange(experts, dtype=jnp.int32) == my_exp).astype(jnp.float32)
    gate_rows = jnp.sum(share_rows * is_mine[None, :], axis=-1, keepdims=True)
    grad_rows = (gate_rows * cotangent_rows).astype(low)
    produced = 0.0
    grad_sent = 0.0
    actives = []
    grad_uppers = []
    for weight_in, weight_out in zip(ins, outs):
        active, derivative = gelu_both(dot(received, weight_in))
        active = active.astype(low)
        grad_upper = (contract_last(grad_rows, weight_out) * derivative).astype(low)
        produced = produced + dot(active, weight_out)
        grad_sent = grad_sent + contract_last(grad_upper, weight_in)
        actives.append(active)
        grad_uppers.append(grad_upper)
    produced_low = produced.astype(low)
    gate_grad_rows = jnp.sum(cotangent_rows * produced_low.astype(jnp.float32), axis=-1)

    def thirds(value):
        first = value.astype(low)
        rest = value - first.astype(jnp.float32)
        second = rest.astype(low)
        third = (rest - second.astype(jnp.float32)).astype(low)
        return jnp.stack([first, second, third], axis=1)

    extra = thirds(gate_grad_rows.reshape(experts, capacity))
    extra = jnp.pad(extra, ((0, 0), (0, 0), (0, width // 3 - capacity))).reshape(experts, 1, width)
    grad_block = jnp.concatenate(
        [grad_sent.astype(low).reshape(experts, capacity, width), extra], axis=1
    )
    grad_block = exchange(grad_block, "exp", n_exp)
    grad_back = unpack(grad_block[:, :capacity].reshape(-1, width))
    gate_parts = grad_block[:, capacity].reshape(experts, 3, width // 3)[:, :, :capacity]
    gate_flat = jnp.sum(gate_parts.astype(jnp.float32), axis=1).reshape(-1)
    gate_grad = jnp.sum(spread.astype(jnp.float32) * gate_flat[:, None], axis=0)

    returned = unpack(
        exchange(produced_low.reshape(experts, capacity, width), "exp", n_exp).reshape(-1, width)
    )
    mixed = (residual + gate[:, None] * returned).astype(low)

    def shared_grad(pieces):
        pieces = [piece.astype(low) for piece in pieces]
        near = pieces[0].astype(jnp.float32) + swap(pieces[1], "tp", n_tp, 1).astype(jnp.float32)
        far = pieces[2].astype(jnp.float32) + swap(pieces[3], "tp", n_tp, 1).astype(jnp.float32)
        return near + swap(far.astype(low), "tp", n_tp, 2).astype(jnp.float32)

    grad_expert_in = shared_grad([contract_first(received, piece) for piece in grad_uppers])[None]
    grad_expert_out = shared_grad([contract_first(piece, grad_rows) for piece in actives])[None]

    upstream = cotangent.astype(jnp.float32)
    logit_grad = ((gate_grad * gate)[:, None] * (choose_float - router_share)).astype(low)
    grad_router = contract_first(mixed_low, logit_grad)
    grad_mixed = contract_last(logit_grad, w_router) + grad_back
    normal = residual * scale_two
    scaled = grad_mixed * ffn_gain
    grad_ffn_gain = jnp.sum(grad_mixed * normal, axis=0)
    grad_residual = upstream + scale_two * (
        scaled - normal * jnp.mean(scaled * normal, axis=-1, keepdims=True)
    )
    grad_low = grad_residual.astype(low)
    grad_whole = both(grad_low, swap(grad_low, "tp", n_tp, 1))

    joint_far, out_far, score_far, normed_far = attend_back(
        kept_far, whole, attended_far, grad_whole, w_joint_far, w_output_far, bias_far
    )
    joint_far = swap(joint_far.astype(low), "tp", n_tp, 2)
    out_far = swap(out_far.astype(low), "tp", n_tp, 2)
    table_far_grad = swap(table_grad(score_far, bias_table.shape[0], length), "tp", n_tp, 2)
    joint_near, out_near, score_near, normed_near = attend_back(
        kept, whole, attended, grad_whole, w_joint, w_output, bias
    )
    grad_normed = normed_near + normed_far
    grad_normed = mine_of(grad_normed) + swap(
        other_of(grad_normed).astype(low), "tp", n_tp, 1
    ).astype(jnp.float32)
    normal = inputs * scale_one
    scaled = grad_normed * attn_gain
    grad_attn_gain = jnp.sum(grad_normed * normal, axis=0)
    grad_tokens = grad_residual + scale_one * (
        scaled - normal * jnp.mean(scaled * normal, axis=-1, keepdims=True)
    )
    grad_table = table_grad(score_near, bias_table.shape[0], length) + table_far_grad
    grad_joint_w = joint_near + joint_far.astype(jnp.float32)
    grad_output_w = out_near + out_far.astype(jnp.float32)
    bits = [1 << place for place in range(n_exp.bit_length() - 1)]
    turned = bits[1:] + bits[:1]
    grad_output_w = wide_sum(grad_output_w, "exp", n_exp, turned)
    half = width // 2
    grad_joint_w = jnp.concatenate(
        [
            wide_sum(grad_joint_w[:half], "exp", n_exp, bits),
            wide_sum(grad_joint_w[half:], "exp", n_exp, turned),
        ],
        axis=0,
    )
    early = jnp.concatenate([grad_ffn_gain[None], grad_router.T], axis=0)
    early = shared_sum(shared_sum(early, "exp", n_exp), "tp", n_tp)
    late = jnp.concatenate([grad_attn_gain, grad_table.reshape(-1)])
    late = shared_sum(late, "exp", n_exp)
    grad_table = late[width:].reshape(grad_table.shape)
    grad_attn_gain = shared_sum(late[:width], "tp", n_tp)
    return (
        mixed,
        grad_tokens,
        grad_attn_gain,
        grad_joint_w[:, :head_width],
        grad_joint_w[:, head_width : 2 * head_width],
        grad_joint_w[:, 2 * head_width :],
        grad_output_w,
        grad_table,
        early[0],
        early[1:].T,
        grad_expert_in,
        grad_expert_out,
    )


def solution(mesh):
    placed = (
        P(("exp", "tp"), None),
        P("exp", None),
        P(("exp", "tp")),
        P(),
        P(None, "tp"),
        P(None, "tp"),
        P(None, "tp"),
        P("tp", None),
        P(None, "tp"),
        P(),
        P(),
        P("exp", None, "tp"),
        P("exp", "tp", None),
        P(("exp", "tp"), None),
    )
    return jax.shard_map(
        functools.partial(local, (mesh.shape["exp"], mesh.shape["tp"])),
        mesh=mesh,
        in_specs=placed,
        out_specs=(
            P(("exp", "tp"), None),
            P(("exp", "tp"), None),
            P(),
            P(None, "tp"),
            P(None, "tp"),
            P(None, "tp"),
            P("tp", None),
            P(None, "tp"),
            P(),
            P(),
            P("exp", None, "tp"),
            P("exp", "tp", None),
        ),
        check_vma=False,
    )
```

```python
import functools

import jax
import jax.numpy as jnp
from jax import lax
from jax.experimental import pallas as pl
from jax.experimental.pallas import tpu as pltpu
from jax.sharding import PartitionSpec as P

HEAD_DIM = 64


EPSILON = 1e-06
MASKED_SCORE = -1000000000.0
thresholds = (8, 12, 16, 23, 32, 46, 64, 91)


def bucket_of(relative):
    distance = jnp.abs(relative)
    distant = 7 + sum(((distance >= boundary).astype(jnp.int32) for boundary in thresholds))
    return jnp.where(distance < 8, distance, distant) + jnp.where(relative > 0, 16, 0)


def bucket_onehot(relative, table_rows):
    return (
        bucket_of(relative)[..., None] == jnp.arange(table_rows, dtype=jnp.int32)
    ).astype(jnp.float32)


def rms_scale(values):
    return lax.rsqrt(jnp.mean(values * values, axis=-1, keepdims=True) + EPSILON)


def dot(left, right):
    return jnp.dot(left, right, preferred_element_type=jnp.float32)


def contract_first(left, right):
    return lax.dot_general(
        left, right, (((0,), (0,)), ((), ())), preferred_element_type=jnp.float32
    )


def contract_last(left, right):
    return lax.dot_general(
        left, right, (((1,), (1,)), ((), ())), preferred_element_type=jnp.float32
    )


def gelu_both(upper):
    slope = 0.7978845608028654
    square = upper * upper
    bend = jnp.tanh(slope * upper * (1.0 + 0.044715 * square))
    half = 0.5 * (1.0 + bend)
    active = upper * half
    derivative = half + 0.5 * upper * (1.0 - bend * bend) * slope * (1.0 + 3 * 0.044715 * square)
    return active, derivative


def swap(value, axis, size, bit):
    return lax.ppermute(value, axis, [(place, place ^ bit) for place in range(size)])


def trade(blocks, axis, size, steps):
    return [swap(blocks[step], axis, size, step) for step in steps]


def trade_all(blocks, axis, size):
    stride = 1
    while stride < size:
        digit = min(8, size // stride)
        shape = blocks.shape
        view = blocks.reshape((size // (stride * digit), digit, stride) + shape[1:])
        parts = [view[:, 0]]
        for step in range(1, digit):
            parts.append(swap(view[:, step], axis, size, step * stride))
        blocks = jnp.stack(parts, axis=1).reshape(shape)
        stride *= digit
    return blocks


def trade_split(blocks, axis, size):
    if size > 8:
        whole = trade_all(blocks, axis, size)
        return [whole], lambda after: [], lambda far, near: far[0]
    far_steps = list(range(size // 2, size))
    near_steps = list(range(1, size // 2))
    far = trade(blocks, axis, size, far_steps)

    def near(held):
        return trade(held, axis, size, near_steps)

    def join(far, near):
        return jnp.stack([blocks[0]] + near + far)

    return far, near, join


def ordered(earlier, later):
    return lax.optimization_barrier((earlier, later))


def shared_sum(value, axis, size):
    bit = 1
    while bit < size:
        value = value + swap(value, axis, size, bit)
        bit *= 2
    return value


def wide_sum(value, axis, size, bits):
    me = lax.axis_index(axis)
    for bit in bits:
        half = value.shape[0] // 2
        side = (me // bit) % 2
        keep = lax.dynamic_slice_in_dim(value, side * half, half, 0)
        send = lax.dynamic_slice_in_dim(value, (1 - side) * half, half, 0)
        value = keep + swap(send.astype(jnp.bfloat16), axis, size, bit).astype(jnp.float32)
    value = value.astype(jnp.bfloat16)
    for bit in reversed(bits):
        other = swap(value, axis, size, bit)
        value = jnp.where(
            (me // bit) % 2 == 0,
            jnp.concatenate([value, other], axis=0),
            jnp.concatenate([other, value], axis=0),
        )
    return value.astype(jnp.float32)


def spread_diagonals(block, rows):
    held = block.shape[0]
    while held < rows:
        block = jnp.concatenate([block, pltpu.roll(block, held, 1)], axis=0)
        held *= 2
    return block


def fold_diagonals(block, rows):
    span = block.shape[1]
    while rows > 8:
        rows //= 2
        block = block[:rows] + pltpu.roll(block[rows:], span - rows, 1)
    return block


def masked_scores(key, query, bias, same):
    scores = contract_first(key, query) + bias
    return jnp.where(same, scores, MASKED_SCORE)


def expert_kernel(
    x_ref,
    g_ref,
    router_ref,
    mine_ref,
    *refs,
):
    weights = refs[:4]
    (
        produced_ref,
        sent_ref,
        grad_rows_ref,
        gate_ref,
        active_ref,
        upper_ref,
        held_ref,
        semaphores,
    ) = refs[4:]
    low = jnp.bfloat16
    width = x_ref.shape[1]
    first = pl.program_id(0) == 0
    copies = [
        pltpu.make_async_copy(weight, held_ref.at[place], semaphores.at[place])
        for place, weight in enumerate(weights)
    ]

    @pl.when(first)
    def _():
        for copy in copies:
            copy.start()

    logits = dot(x_ref[...], router_ref[...])
    logits = logits - jnp.max(logits, axis=1, keepdims=True)
    unscaled = jnp.exp(logits)
    gate = jnp.sum(unscaled * mine_ref[...], axis=1, keepdims=True) / jnp.sum(
        unscaled, axis=1, keepdims=True
    )
    grad_rows = (gate * g_ref[...].astype(jnp.float32)).astype(low)
    grad_rows_ref[...] = grad_rows
    produced = jnp.zeros(x_ref.shape, jnp.float32)
    sent = jnp.zeros(x_ref.shape, jnp.float32)
    for place, copy in enumerate(copies):

        @pl.when(first)
        def _():
            copy.wait()

        weight_in = held_ref[place, pl.ds(0, width)]
        weight_out = held_ref[place, pl.ds(width, width)]
        columns = pl.ds(place * width, width)
        active, derivative = gelu_both(dot(x_ref[...], weight_in))
        active = active.astype(low)
        upper = (contract_last(grad_rows, weight_out) * derivative).astype(low)
        active_ref[:, columns] = active
        upper_ref[:, columns] = upper
        produced = produced + dot(active, weight_out)
        sent = sent + contract_last(upper, weight_in)
    produced = produced.astype(low)
    produced_ref[...] = produced
    sent_ref[...] = sent.astype(low)
    gate_ref[...] = jnp.sum(
        g_ref[...].astype(jnp.float32) * produced.astype(jnp.float32), axis=1, keepdims=True
    )


def expert_pass(received, cotangent_rows, w_router, my_expert, weights):
    rows, width = received.shape
    experts = w_router.shape[1]
    tile = 240
    hidden = width * len(weights)
    low = jnp.bfloat16
    is_mine = (jnp.arange(experts, dtype=jnp.int32) == my_expert).astype(jnp.float32)[None, :]
    tiled = lambda columns: pl.BlockSpec((tile, columns), lambda i: (i, 0))
    fixed = lambda *shape: pl.BlockSpec(shape, lambda i: (0,) * len(shape))
    shape = lambda columns, dtype: jax.ShapeDtypeStruct((rows, columns), dtype)
    return pl.pallas_call(
        expert_kernel,
        grid=(rows // tile,),
        in_specs=[tiled(width), tiled(width), fixed(width, experts), fixed(1, experts)]
        + [pl.BlockSpec(memory_space=pl.ANY)] * len(weights),
        out_specs=[
            tiled(width),
            tiled(width),
            tiled(width),
            tiled(1),
            tiled(hidden),
            tiled(hidden),
        ],
        out_shape=[
            shape(width, low),
            shape(width, low),
            shape(width, low),
            shape(1, jnp.float32),
            shape(hidden, low),
            shape(hidden, low),
        ],
        scratch_shapes=[
            pltpu.VMEM((len(weights), 2 * width, width), low),
            pltpu.SemaphoreType.DMA((len(weights),)),
        ],
        compiler_params=pltpu.CompilerParams(vmem_limit_bytes=48 * 1024 * 1024),
        cost_estimate=pl.CostEstimate(
            flops=rows * width * hidden * 8,
            bytes_accessed=rows * hidden * 4 + width * hidden * 4,
            transcendentals=rows * hidden,
        ),
        name="expert_pass",
    )(received, cotangent_rows, w_router, is_mine, *weights)


def outer_kernel(x_ref, upper_ref, active_ref, grad_ref, out_ref):
    width = x_ref.shape[1]
    out_ref[0, pl.ds(0, width)] = contract_first(x_ref[...], upper_ref[...]).astype(out_ref.dtype)
    out_ref[0, pl.ds(width, width)] = contract_first(active_ref[...], grad_ref[...]).astype(
        out_ref.dtype
    )


def expert_outer(received, grad_upper, active, grad_rows, first, dtype):
    rows, width = received.shape
    count = active.shape[1] // width // 2
    fixed = pl.BlockSpec((rows, width), lambda i: (0, 0))
    some = pl.BlockSpec((rows, width), lambda i: (0, 2 * i + first))
    return pl.pallas_call(
        outer_kernel,
        grid=(count,),
        in_specs=[fixed, some, some, fixed],
        out_specs=pl.BlockSpec((1, 2 * width, width), lambda i: (i, 0, 0)),
        out_shape=jax.ShapeDtypeStruct((count, 2 * width, width), dtype),
        compiler_params=pltpu.CompilerParams(vmem_limit_bytes=48 * 1024 * 1024),
        cost_estimate=pl.CostEstimate(
            flops=rows * width * width * 4 * count,
            bytes_accessed=rows * width * 8 + count * width * width * 8,
            transcendentals=0,
        ),
        name="expert_outer",
    )(received, grad_upper, active, grad_rows)


def attend_kernel(
    heads, chunk, has_base, x_ref, w_ref, w_out_ref, base_ref, row_ref, column_ref, *refs
):
    if has_base:
        given_ref, joint_ref, attended_ref, log_ref, partial_ref, bias_ref = refs
    else:
        joint_ref, attended_ref, log_ref, partial_ref, bias_ref = refs
    low = jnp.bfloat16
    length = x_ref.shape[0]
    width = heads * HEAD_DIM

    @pl.when(pl.program_id(0) == 0)
    def _():
        for head in range(heads):
            bias_ref[head] = spread_diagonals(base_ref[head], length)[:, :length]

    joint_ref[0] = contract_last(w_ref[...], x_ref[...]).astype(low)
    for head in range(heads):
        first = head * HEAD_DIM
        here = pl.ds(first, HEAD_DIM)
        key = joint_ref[0, pl.ds(width + first, HEAD_DIM)]
        value = joint_ref[0, pl.ds(2 * width + first, HEAD_DIM)]
        for start in range(0, length, chunk):
            some = pl.ds(start, chunk)
            same = column_ref[0] == row_ref[0, :, some]
            masked = masked_scores(key, joint_ref[0, here, some], bias_ref[head, :, some], same)
            peak = jnp.max(masked, axis=0, keepdims=True)
            unscaled = jnp.exp(masked - peak)
            total = jnp.sum(unscaled, axis=0, keepdims=True)
            weight_low = (unscaled * (1.0 / total)).astype(low)
            log_ref[0, pl.ds(head, 1), some] = peak + jnp.log(total)
            attended_ref[0, here, some] = dot(value, weight_low).astype(low)
    partial = contract_first(attended_ref[0], w_out_ref[...])
    if has_base:
        partial = partial + given_ref[...]
    partial_ref[...] = partial


def attend(whole, segments, w_joint, w_out, base, given):
    seq_count, length = segments.shape
    total, width = whole.shape
    joint_width = w_joint.shape[0]
    head_width = joint_width // 3
    heads = head_width // HEAD_DIM
    chunk = min(length, 256)
    f32, low = jnp.float32, jnp.bfloat16
    fixed = lambda *shape: pl.BlockSpec(shape, lambda i: (0,) * len(shape))
    each = lambda *shape: pl.BlockSpec((1,) + shape, lambda i: (i, 0, 0))
    rows = pl.BlockSpec((length, width), lambda i: (i, 0))
    operands = [
        whole,
        w_joint,
        w_out,
        base,
        segments[:, None, :],
        segments[:, :, None],
    ]
    specs = [
        rows,
        fixed(joint_width, width),
        fixed(head_width, width),
        fixed(heads, 8, base.shape[2]),
        each(1, length),
        each(length, 1),
    ]
    if given is not None:
        operands.append(given)
        specs.append(rows)
    pairs = seq_count * heads * length * length
    return pl.pallas_call(
        functools.partial(attend_kernel, heads, chunk, given is not None),
        grid=(seq_count,),
        in_specs=specs,
        out_specs=[
            each(joint_width, length),
            each(head_width, length),
            each(8, length),
            rows,
        ],
        out_shape=[
            jax.ShapeDtypeStruct((seq_count, joint_width, length), low),
            jax.ShapeDtypeStruct((seq_count, head_width, length), low),
            jax.ShapeDtypeStruct((seq_count, 8, length), f32),
            jax.ShapeDtypeStruct((total, width), f32),
        ],
        scratch_shapes=[pltpu.VMEM((heads, length, length), f32)],
        compiler_params=pltpu.CompilerParams(vmem_limit_bytes=48 * 1024 * 1024),
        cost_estimate=pl.CostEstimate(
            flops=pairs * HEAD_DIM * 16 + total * width * head_width * 8,
            bytes_accessed=total * width * 8 + joint_width * width * 4,
            transcendentals=pairs,
        ),
        name="attend",
    )(*operands)


def attend_back_kernel(
    heads,
    chunk,
    has_base,
    x_ref,
    g_ref,
    w_ref,
    w_out_ref,
    base_ref,
    row_ref,
    column_ref,
    joint_ref,
    attended_ref,
    log_ref,
    *refs,
):
    if has_base:
        given_ref, *refs = refs
    (
        w_grad_ref,
        w_out_grad_ref,
        table_ref,
        normed_ref,
        bias_ref,
        total_ref,
        back_ref,
        grad_ref,
    ) = refs
    low = jnp.bfloat16
    length = x_ref.shape[0]
    width = heads * HEAD_DIM
    span = base_ref.shape[2]

    @pl.when(pl.program_id(0) == 0)
    def _():
        for head in range(heads):
            bias_ref[head] = spread_diagonals(base_ref[head], length)[:, :length]
        total_ref[...] = jnp.zeros_like(total_ref)
        w_grad_ref[...] = jnp.zeros_like(w_grad_ref)
        w_out_grad_ref[...] = jnp.zeros_like(w_out_grad_ref)

    w_out_grad_ref[...] += dot(attended_ref[0], g_ref[...])
    back_ref[...] = contract_last(w_out_ref[...], g_ref[...]).astype(low)
    for head in range(heads):
        first = head * HEAD_DIM
        here = pl.ds(first, HEAD_DIM)
        key = joint_ref[0, pl.ds(width + first, HEAD_DIM)]
        value = joint_ref[0, pl.ds(2 * width + first, HEAD_DIM)]
        grad_key = 0.0
        grad_value = 0.0
        for start in range(0, length, chunk):
            some = pl.ds(start, chunk)
            query = joint_ref[0, here, some]
            back = back_ref[here, some]
            same = column_ref[0] == row_ref[0, :, some]
            masked = masked_scores(key, query, bias_ref[head, :, some], same)
            weight = jnp.exp(masked - log_ref[0, pl.ds(head, 1), some])
            grad_weight = contract_first(value, back)
            grad_value = grad_value + contract_last(back, weight.astype(low))
            delta = jnp.sum(weight * grad_weight, axis=0, keepdims=True)
            grad_scores = (weight * (grad_weight - delta)).astype(low)
            total_ref[head, :, some] += grad_scores.astype(jnp.float32)
            grad_key = grad_key + contract_last(query, grad_scores)
            grad_ref[here, some] = dot(key, grad_scores).astype(low)
        grad_ref[pl.ds(width + first, HEAD_DIM), :] = grad_key.astype(low)
        grad_ref[pl.ds(2 * width + first, HEAD_DIM), :] = grad_value.astype(low)
    w_grad_ref[...] += dot(grad_ref[...], x_ref[...])
    normed = contract_first(grad_ref[...], w_ref[...])
    if has_base:
        normed = normed + given_ref[...]
    normed_ref[...] = normed

    @pl.when(pl.program_id(0) == pl.num_programs(0) - 1)
    def _():
        for head in range(heads):
            padded = jnp.concatenate(
                [total_ref[head], jnp.zeros((length, span - length), jnp.float32)], axis=1
            )
            table_ref[head] = fold_diagonals(padded, length)


def attend_back(kept, whole, grad_whole, segments, w_joint, w_out, base, given):
    joint, attended, logs = kept
    seq_count, length = segments.shape
    total, width = whole.shape
    joint_width = w_joint.shape[0]
    head_width = joint_width // 3
    heads = head_width // HEAD_DIM
    chunk = min(length, 256)
    f32, low = jnp.float32, jnp.bfloat16
    fixed = lambda *shape: pl.BlockSpec(shape, lambda i: (0,) * len(shape))
    each = lambda *shape: pl.BlockSpec((1,) + shape, lambda i: (i, 0, 0))
    rows = pl.BlockSpec((length, width), lambda i: (i, 0))
    operands = [
        whole,
        grad_whole,
        w_joint,
        w_out,
        base,
        segments[:, None, :],
        segments[:, :, None],
        joint,
        attended,
        logs,
    ]
    specs = [
        rows,
        rows,
        fixed(joint_width, width),
        fixed(head_width, width),
        fixed(heads, 8, base.shape[2]),
        each(1, length),
        each(length, 1),
        each(joint_width, length),
        each(head_width, length),
        each(8, length),
    ]
    if given is not None:
        operands.append(given)
        specs.append(rows)
    pairs = seq_count * heads * length * length
    return pl.pallas_call(
        functools.partial(attend_back_kernel, heads, chunk, given is not None),
        grid=(seq_count,),
        in_specs=specs,
        out_specs=[
            fixed(joint_width, width),
            fixed(head_width, width),
            fixed(heads, 8, base.shape[2]),
            rows,
        ],
        out_shape=[
            jax.ShapeDtypeStruct((joint_width, width), f32),
            jax.ShapeDtypeStruct((head_width, width), f32),
            jax.ShapeDtypeStruct((heads, 8, base.shape[2]), f32),
            jax.ShapeDtypeStruct((total, width), f32),
        ],
        scratch_shapes=[
            pltpu.VMEM((heads, length, length), f32),
            pltpu.VMEM((heads, length, length), f32),
            pltpu.VMEM((head_width, length), low),
            pltpu.VMEM((joint_width, length), low),
        ],
        compiler_params=pltpu.CompilerParams(vmem_limit_bytes=56 * 1024 * 1024),
        cost_estimate=pl.CostEstimate(
            flops=pairs * HEAD_DIM * 40 + total * width * head_width * 16,
            bytes_accessed=total * width * 16 + joint_width * width * 8,
            transcendentals=pairs,
        ),
        name="attend_back",
    )(*operands)


def bias_base(table, length):
    span = 2 * length
    offset = jnp.arange(span, dtype=jnp.int32)[None, :] - jnp.arange(8, dtype=jnp.int32)[:, None]
    offset = jnp.where(offset < 0, offset + span, offset)
    relative = jnp.where(offset < length, -offset, span - offset)
    onehot = bucket_onehot(relative, table.shape[0])
    return jnp.einsum("stb,bh->hst", onehot, table, precision=lax.Precision.HIGHEST)


def table_grad(folded, table_rows, length):
    span = 2 * length
    offset = jnp.arange(span, dtype=jnp.int32)[None, :] - jnp.arange(8, dtype=jnp.int32)[:, None]
    offset = jnp.where(offset < 0, offset + span, offset)
    relative = jnp.where(offset < length, -offset, span - offset)
    onehot = bucket_onehot(relative, table_rows)
    return jnp.einsum("stb,hst->bh", onehot, folded, precision=lax.Precision.HIGHEST)


def local(
    sizes,
    tokens,
    segments,
    routes,
    attn_gain,
    w_query,
    w_key,
    w_value,
    w_output,
    bias_table,
    ffn_gain,
    w_router,
    expert_in,
    expert_out,
    cotangent,
):
    n_exp, n_tp = sizes
    rows, width = tokens.shape
    group_seqs, length = segments.shape
    head_width = w_query.shape[1]
    experts = w_router.shape[1]
    capacity = rows * 5 // (4 * experts)
    low = jnp.bfloat16
    my_exp = lax.axis_index("exp")
    my_tp = lax.axis_index("tp")
    my_core = my_tp % 2
    pair_seqs = group_seqs * 2 // n_tp
    seqs = lax.dynamic_slice_in_dim(segments, (my_tp // 2) * pair_seqs, pair_seqs, 0)

    def both(mine, other):
        return jnp.where(
            my_core == 0,
            jnp.concatenate([mine, other], axis=0),
            jnp.concatenate([other, mine], axis=0),
        )

    def mine_of(pair):
        return lax.dynamic_slice_in_dim(pair, my_core * rows, rows, 0)

    def other_of(pair):
        return lax.dynamic_slice_in_dim(pair, (1 - my_core) * rows, rows, 0)

    joint_width = 3 * head_width
    w_attn = jnp.concatenate([w_query.T, w_key.T, w_value.T, w_output], axis=0)
    w_attn_far = swap(w_attn, "tp", n_tp, 2)
    w_joint, w_out = w_attn[:joint_width], w_attn[joint_width:]
    expert_both = jnp.concatenate([expert_in[0], expert_out[0]], axis=0)
    w_attn_far, expert_both = ordered(w_attn_far, expert_both)
    w_joint_far, w_out_far = w_attn_far[:joint_width], w_attn_far[joint_width:]
    base = bias_base(bias_table, length)
    base_far = bias_base(swap(bias_table, "tp", n_tp, 2), length)

    place = jnp.arange(rows, dtype=jnp.int32)
    choose = routes[:, None] == jnp.arange(experts, dtype=jnp.int32)[None, :]
    choose_float = choose.astype(jnp.float32)
    rank = dot((place[:, None] > place[None, :]).astype(low), choose.astype(low))
    slot = jnp.sum(rank * choose_float, axis=-1).astype(jnp.int32)
    target = jnp.where(slot < capacity, (routes ^ my_exp) * capacity + slot, experts * capacity)
    spread = (
        target[None, :] == jnp.arange(experts * capacity, dtype=jnp.int32)[:, None]
    ).astype(low)

    def pack(data):
        return dot(spread, data).astype(low).reshape(experts, capacity, width)

    def unpack(data):
        return contract_first(spread, data)

    packed_cotangent = pack(cotangent)
    cotangent_far, cotangent_near, cotangent_join = trade_split(packed_cotangent, "exp", n_exp)

    inputs = tokens.astype(jnp.float32)
    scale_one = rms_scale(inputs)
    normed_low = (inputs * scale_one * attn_gain).astype(low)
    whole = both(normed_low, swap(normed_low, "tp", n_tp, 1))
    *kept, partial = attend(whole, seqs, w_joint, w_out, base, None)
    partial, packed_cotangent = ordered(partial, packed_cotangent)
    cotangent_far, partial = ordered(cotangent_far, partial)
    cotangent_near = cotangent_near(packed_cotangent)

    expert_far = swap(expert_both, "tp", n_tp, 2)
    expert_near = swap(expert_both, "tp", n_tp, 1)

    *kept_far, partial = attend(whole, seqs, w_joint_far, w_out_far, base_far, partial)
    residual = inputs + (mine_of(partial) + swap(other_of(partial).astype(low), "tp", n_tp, 1))

    scale_two = rms_scale(residual)
    mixed_low = (residual * scale_two * ffn_gain).astype(low)
    router_share = jax.nn.softmax(dot(mixed_low, w_router), axis=-1)
    gate = jnp.sum(router_share * choose_float, axis=-1)
    cotangent_sent = cotangent_join(cotangent_far, cotangent_near)
    (cotangent_sent, expert_near), packed = ordered(
        (cotangent_sent, expert_near), pack(mixed_low)
    )
    far, near, join = trade_split(packed, "exp", n_exp)
    near = near(packed)
    far[:2], expert_far = ordered(far[:2], expert_far)
    received = join(far, near).reshape(-1, width)
    expert_all = [expert_both, expert_near, expert_far, swap(expert_far, "tp", n_tp, 1)]

    produced_low, grad_sent, grad_rows, gate_grad_rows, active, grad_upper = expert_pass(
        received, cotangent_sent.reshape(-1, width), w_router, my_exp, expert_all
    )

    def thirds(value):
        first = value.astype(low)
        rest = value - first.astype(jnp.float32)
        second = rest.astype(low)
        third = (rest - second.astype(jnp.float32)).astype(low)
        return jnp.stack([first, second, third], axis=1)

    extra = thirds(gate_grad_rows.reshape(experts, capacity))
    extra = jnp.pad(extra, ((0, 0), (0, 0), (0, width // 3 - capacity))).reshape(experts, 1, width)
    grad_block = jnp.concatenate(
        [grad_sent.reshape(experts, capacity, width), extra], axis=1
    )
    far, near, join = trade_split(grad_block, "exp", n_exp)
    near = near(grad_block)
    if near:
        near[0], (received, grad_rows) = ordered(near[0], (received, grad_rows))

    pieces = (received, grad_upper, active, grad_rows)
    outer_send = expert_outer(*pieces, 1, low)
    outer_send, pieces = ordered(outer_send, pieces)
    outer_keep = expert_outer(*pieces, 0, jnp.float32)
    outer_keep, (far, near) = ordered(outer_keep, (far, near))
    grad_block = join(far, near)
    summed = outer_keep + swap(outer_send, "tp", n_tp, 1).astype(jnp.float32)
    grad_back = unpack(grad_block[:, :capacity].reshape(-1, width))
    gate_parts = grad_block[:, capacity].reshape(experts, 3, width // 3)[:, :, :capacity]
    gate_flat = jnp.sum(gate_parts.astype(jnp.float32), axis=1).reshape(-1)
    gate_grad = jnp.sum(spread.astype(jnp.float32) * gate_flat[:, None], axis=0)

    upstream = cotangent.astype(jnp.float32)
    logit_grad = ((gate_grad * gate)[:, None] * (choose_float - router_share)).astype(low)
    grad_router = contract_first(mixed_low, logit_grad)
    grad_mixed = contract_last(logit_grad, w_router) + grad_back
    normal = residual * scale_two
    scaled = grad_mixed * ffn_gain
    grad_ffn_gain = jnp.sum(grad_mixed * normal, axis=0)
    grad_residual = upstream + scale_two * (
        scaled - normal * jnp.mean(scaled * normal, axis=-1, keepdims=True)
    )
    grad_low = grad_residual.astype(low)
    grad_whole = both(grad_low, swap(grad_low, "tp", n_tp, 1))

    summed, grad_whole = ordered(summed, grad_whole)
    across = summed[1].astype(low)
    across_in = swap(across[:width], "tp", n_tp, 2)
    grad_whole, produced_low = ordered(grad_whole, produced_low)
    produced_low = produced_low.reshape(experts, capacity, width)
    far, near, join = trade_split(produced_low, "exp", n_exp)

    joint_far, out_far, folded_far, grad_normed = attend_back(
        kept_far, whole, grad_whole, seqs, w_joint_far, w_out_far, base_far, None
    )
    joint_far, produced_low = ordered(joint_far, produced_low)
    (far, across_in), grad_normed = ordered((far, across_in), grad_normed)
    near = near(produced_low)
    across_out = swap(across[width:], "tp", n_tp, 2)
    grad_expert_in = (summed[0, :width] + across_in.astype(jnp.float32))[None]
    grad_expert_out = (summed[0, width:] + across_out.astype(jnp.float32))[None]
    grad_attn_far = swap(
        jnp.concatenate([joint_far.astype(low), out_far.astype(low)], axis=0), "tp", n_tp, 2
    )
    table_rows = bias_table.shape[0]
    table_far = swap(table_grad(folded_far, table_rows, length), "tp", n_tp, 2)
    joint_near, out_near, folded, grad_normed = attend_back(
        kept, whole, grad_whole, seqs, w_joint, w_out, base, grad_normed
    )
    grad_normed, near = ordered(grad_normed, near)
    returned = unpack(join(far, near).reshape(-1, width))
    mixed = (residual + gate[:, None] * returned).astype(low)
    grad_normed = mine_of(grad_normed) + swap(
        other_of(grad_normed).astype(low), "tp", n_tp, 1
    ).astype(jnp.float32)
    normal = inputs * scale_one
    scaled = grad_normed * attn_gain
    grad_attn_gain = jnp.sum(grad_normed * normal, axis=0)
    grad_tokens = grad_residual + scale_one * (
        scaled - normal * jnp.mean(scaled * normal, axis=-1, keepdims=True)
    )
    grad_table = table_grad(folded, table_rows, length) + table_far
    grad_attn = jnp.concatenate([joint_near, out_near], axis=0) + grad_attn_far.astype(jnp.float32)
    bits = [1 << place for place in range(n_exp.bit_length() - 1)]
    turned = bits[1:] + bits[:1]
    half = grad_attn.shape[0] // 2
    grad_attn = jnp.concatenate(
        [
            wide_sum(grad_attn[:half], "exp", n_exp, bits),
            wide_sum(grad_attn[half:], "exp", n_exp, turned),
        ],
        axis=0,
    )
    small = jnp.concatenate(
        [grad_attn_gain, grad_ffn_gain, grad_router.T.reshape(-1), grad_table.reshape(-1)]
    )
    small = shared_sum(small, "exp", n_exp)
    grad_table = small[(2 + experts) * width :].reshape(grad_table.shape)
    small = shared_sum(small[: (2 + experts) * width], "tp", n_tp).reshape(-1, width)
    return (
        mixed,
        grad_tokens,
        small[0],
        grad_attn[:head_width].T,
        grad_attn[head_width : 2 * head_width].T,
        grad_attn[2 * head_width : joint_width].T,
        grad_attn[joint_width:],
        grad_table,
        small[1],
        small[2:].T,
        grad_expert_in,
        grad_expert_out,
    )


def solution(mesh):
    placed = (
        P(("exp", "tp"), None),
        P("exp", None),
        P(("exp", "tp")),
        P(),
        P(None, "tp"),
        P(None, "tp"),
        P(None, "tp"),
        P("tp", None),
        P(None, "tp"),
        P(),
        P(),
        P("exp", None, "tp"),
        P("exp", "tp", None),
        P(("exp", "tp"), None),
    )
    return jax.shard_map(
        functools.partial(local, (mesh.shape["exp"], mesh.shape["tp"])),
        mesh=mesh,
        in_specs=placed,
        out_specs=(
            P(("exp", "tp"), None),
            P(("exp", "tp"), None),
            P(),
            P(None, "tp"),
            P(None, "tp"),
            P(None, "tp"),
            P("tp", None),
            P(None, "tp"),
            P(),
            P(),
            P("exp", None, "tp"),
            P("exp", "tp", None),
        ),
        check_vma=False,
    )
```

```python
import functools
import math

import jax
import jax.numpy as jnp
from jax import lax
from jax.experimental import pallas as pl
from jax.experimental.pallas import tpu as pltpu
from jax.sharding import PartitionSpec as P

HEAD_DIM = 64


EPSILON = 1e-06
MASKED_SCORE = -1000000000.0
thresholds = (8, 12, 16, 23, 32, 46, 64, 91)


def bucket_of(relative):
    distance = jnp.abs(relative)
    distant = 7 + sum(((distance >= boundary).astype(jnp.int32) for boundary in thresholds))
    return jnp.where(distance < 8, distance, distant) + jnp.where(relative > 0, 16, 0)


def bucket_onehot(relative, table_rows):
    return (
        bucket_of(relative)[..., None] == jnp.arange(table_rows, dtype=jnp.int32)
    ).astype(jnp.float32)


def rms_scale(values):
    return lax.rsqrt(jnp.mean(values * values, axis=-1, keepdims=True) + EPSILON)


def dot(left, right):
    return jnp.dot(left, right, preferred_element_type=jnp.float32)


def contract_first(left, right):
    return lax.dot_general(
        left, right, (((0,), (0,)), ((), ())), preferred_element_type=jnp.float32
    )


def contract_last(left, right):
    return lax.dot_general(
        left, right, (((1,), (1,)), ((), ())), preferred_element_type=jnp.float32
    )


def gelu_both(upper):
    slope = 0.7978845608028654
    square = upper * upper
    bend = jnp.tanh(slope * upper * (1.0 + 0.044715 * square))
    half = 0.5 * (1.0 + bend)
    active = upper * half
    derivative = half + 0.5 * upper * (1.0 - bend * bend) * slope * (1.0 + 3 * 0.044715 * square)
    return active, derivative


def swap(value, axis, size, bit):
    return lax.ppermute(value, axis, [(place, place ^ bit) for place in range(size)])


def trade_all(blocks, axis, size):
    stride = 1
    while stride < size:
        digit = min(8, size // stride)
        shape = blocks.shape
        view = blocks.reshape((size // (stride * digit), digit, stride) + shape[1:])
        parts = [view[:, 0]]
        for step in range(1, digit):
            parts.append(swap(view[:, step], axis, size, step * stride))
        blocks = jnp.stack(parts, axis=1).reshape(shape)
        stride *= digit
    return blocks


def first_wave(blocks, axis, size, steps):
    if size > 8:
        whole = trade_all(blocks, axis, size)
        return {step: whole[step] for step in range(1, size)}
    return {step: swap(blocks[step], axis, size, step) for step in steps if step < size}


def next_wave(blocks, axis, size, steps):
    if size > 8:
        return {}
    return {step: swap(blocks[step], axis, size, step) for step in steps if step < size}


def join(blocks, *waves):
    got = {0: blocks[0]}
    for wave in waves:
        got.update(wave)
    return jnp.stack([got[step] for step in range(blocks.shape[0])])


def chosen(wave, steps):
    return {step: wave[step] for step in steps if step in wave}


def ordered(earlier, later):
    return lax.optimization_barrier((earlier, later))


def halve(value, axis, size, bit):
    side = (lax.axis_index(axis) // bit) % 2
    half = value.shape[0] // 2
    keep = lax.dynamic_slice_in_dim(value, side * half, half, 0)
    send = lax.dynamic_slice_in_dim(value, (1 - side) * half, half, 0)
    return keep + swap(send.astype(jnp.bfloat16), axis, size, bit).astype(jnp.float32)


def double(value, axis, size, bit):
    other = swap(value, axis, size, bit)
    return jnp.where(
        (lax.axis_index(axis) // bit) % 2 == 0,
        jnp.concatenate([value, other], axis=0),
        jnp.concatenate([other, value], axis=0),
    )


def spread_diagonals(block, rows):
    held = block.shape[0]
    while held < rows:
        block = jnp.concatenate([block, pltpu.roll(block, held, 1)], axis=0)
        held *= 2
    return block


def fold_diagonals(block, rows):
    span = block.shape[1]
    while rows > 8:
        rows //= 2
        block = block[:rows] + pltpu.roll(block[rows:], span - rows, 1)
    return block


def masked_scores(key, query, bias, same):
    scores = contract_first(key, query) + bias
    return jnp.where(same, scores, MASKED_SCORE)


def expert_kernel(
    x_ref,
    g_ref,
    router_ref,
    mine_ref,
    *refs,
):
    weights = refs[:4]
    (
        produced_ref,
        sent_ref,
        grad_rows_ref,
        gate_ref,
        active_ref,
        upper_ref,
        held_ref,
        semaphores,
    ) = refs[4:]
    low = jnp.bfloat16
    width = x_ref.shape[1]
    first = pl.program_id(0) == 0
    copies = [
        pltpu.make_async_copy(weight, held_ref.at[place], semaphores.at[place])
        for place, weight in enumerate(weights)
    ]

    @pl.when(first)
    def _():
        for copy in copies:
            copy.start()

    logits = dot(x_ref[...], router_ref[...])
    logits = logits - jnp.max(logits, axis=1, keepdims=True)
    unscaled = jnp.exp(logits)
    gate = jnp.sum(unscaled * mine_ref[...], axis=1, keepdims=True) / jnp.sum(
        unscaled, axis=1, keepdims=True
    )
    grad_rows = (gate * g_ref[...].astype(jnp.float32)).astype(low)
    grad_rows_ref[...] = grad_rows
    produced = jnp.zeros(x_ref.shape, jnp.float32)
    sent = jnp.zeros(x_ref.shape, jnp.float32)
    for place, copy in enumerate(copies):

        @pl.when(first)
        def _():
            copy.wait()

        weight_in = held_ref[place, pl.ds(0, width)]
        weight_out = held_ref[place, pl.ds(width, width)]
        columns = pl.ds(place * width, width)
        active, derivative = gelu_both(dot(x_ref[...], weight_in))
        active = active.astype(low)
        upper = (contract_last(grad_rows, weight_out) * derivative).astype(low)
        active_ref[:, columns] = active
        upper_ref[:, columns] = upper
        produced = produced + dot(active, weight_out)
        sent = sent + contract_last(upper, weight_in)
    produced = produced.astype(low)
    produced_ref[...] = produced
    sent_ref[...] = sent.astype(low)
    gate_ref[...] = jnp.sum(
        g_ref[...].astype(jnp.float32) * produced.astype(jnp.float32), axis=1, keepdims=True
    )


def expert_pass(received, cotangent_rows, w_router, my_expert, weights):
    rows, width = received.shape
    experts = w_router.shape[1]
    tile = 240
    hidden = width * len(weights)
    low = jnp.bfloat16
    is_mine = (jnp.arange(experts, dtype=jnp.int32) == my_expert).astype(jnp.float32)[None, :]
    tiled = lambda columns: pl.BlockSpec((tile, columns), lambda i: (i, 0))
    fixed = lambda *shape: pl.BlockSpec(shape, lambda i: (0,) * len(shape))
    shape = lambda columns, dtype: jax.ShapeDtypeStruct((rows, columns), dtype)
    return pl.pallas_call(
        expert_kernel,
        grid=(rows // tile,),
        in_specs=[tiled(width), tiled(width), fixed(width, experts), fixed(1, experts)]
        + [pl.BlockSpec(memory_space=pl.ANY)] * len(weights),
        out_specs=[
            tiled(width),
            tiled(width),
            tiled(width),
            tiled(1),
            tiled(hidden),
            tiled(hidden),
        ],
        out_shape=[
            shape(width, low),
            shape(width, low),
            shape(width, low),
            shape(1, jnp.float32),
            shape(hidden, low),
            shape(hidden, low),
        ],
        scratch_shapes=[
            pltpu.VMEM((len(weights), 2 * width, width), low),
            pltpu.SemaphoreType.DMA((len(weights),)),
        ],
        compiler_params=pltpu.CompilerParams(vmem_limit_bytes=48 * 1024 * 1024),
        cost_estimate=pl.CostEstimate(
            flops=rows * width * hidden * 8,
            bytes_accessed=rows * hidden * 4 + width * hidden * 4,
            transcendentals=rows * hidden,
        ),
        name="expert_pass",
    )(received, cotangent_rows, w_router, is_mine, *weights)


def outer_kernel(x_ref, upper_ref, active_ref, grad_ref, out_ref):
    width = x_ref.shape[1]
    out_ref[0, pl.ds(0, width)] = contract_first(x_ref[...], upper_ref[...]).astype(out_ref.dtype)
    out_ref[0, pl.ds(width, width)] = contract_first(active_ref[...], grad_ref[...]).astype(
        out_ref.dtype
    )


def expert_outer(received, grad_upper, active, grad_rows, first, dtype):
    rows, width = received.shape
    count = active.shape[1] // width // 2
    fixed = pl.BlockSpec((rows, width), lambda i: (0, 0))
    some = pl.BlockSpec((rows, width), lambda i: (0, 2 * i + first))
    return pl.pallas_call(
        outer_kernel,
        grid=(count,),
        in_specs=[fixed, some, some, fixed],
        out_specs=pl.BlockSpec((1, 2 * width, width), lambda i: (i, 0, 0)),
        out_shape=jax.ShapeDtypeStruct((count, 2 * width, width), dtype),
        compiler_params=pltpu.CompilerParams(vmem_limit_bytes=48 * 1024 * 1024),
        cost_estimate=pl.CostEstimate(
            flops=rows * width * width * 4 * count,
            bytes_accessed=rows * width * 8 + count * width * width * 8,
            transcendentals=0,
        ),
        name="expert_outer",
    )(received, grad_upper, active, grad_rows)


def sequence_rows(core_ref, pieces, per, held_ref):
    half = pieces[0].shape[0]
    for part in range(len(pieces) // 2):
        place = pl.program_id(0) * (len(pieces) // 2) + part
        is_mine = (place >= per) == (core_ref[0] == 1)

        @pl.when(is_mine)
        def _():
            held_ref[pl.ds(part * half, half)] = pieces[2 * part][...]

        @pl.when(jnp.logical_not(is_mine))
        def _():
            held_ref[pl.ds(part * half, half)] = pieces[2 * part + 1][...]


def part_rows(core_ref, value, per, keep_ref, send_ref):
    half = keep_ref.shape[0] // per
    count = value.shape[0] // half
    for part in range(count):
        place = pl.program_id(0) * count + part
        is_mine = (place >= per) == (core_ref[0] == 1)
        here = pl.ds(pl.multiple_of((place % per) * half, half), half)
        some = value[part * half : (part + 1) * half]

        @pl.when(is_mine)
        def _():
            keep_ref[here] = some

        @pl.when(jnp.logical_not(is_mine))
        def _():
            send_ref[here] = some.astype(send_ref.dtype)


def attend_kernel(heads, chunk, per, parts, last, core_ref, *refs):
    pieces, refs = refs[: 2 * parts], refs[2 * parts :]
    w_ref, base_ref, row_ref, column_ref, *refs = refs
    if last:
        given_ref, joint_ref, attended_ref, log_ref, keep_ref, send_ref, bias_ref, x_ref = refs
    else:
        joint_ref, attended_ref, log_ref, partial_ref, bias_ref, x_ref = refs
    low = jnp.bfloat16
    length = x_ref.shape[0]
    width = heads * HEAD_DIM

    @pl.when(pl.program_id(0) == 0)
    def _():
        for head in range(heads):
            bias_ref[head] = spread_diagonals(base_ref[head], length)[:, :length]

    sequence_rows(core_ref, pieces, per, x_ref)
    joint_ref[0] = contract_last(w_ref[pl.ds(0, 3 * width)], x_ref[...]).astype(low)
    for head in range(heads):
        first = head * HEAD_DIM
        here = pl.ds(first, HEAD_DIM)
        key = joint_ref[0, pl.ds(width + first, HEAD_DIM)]
        value = joint_ref[0, pl.ds(2 * width + first, HEAD_DIM)]
        for start in range(0, length, chunk):
            some = pl.ds(start, chunk)
            same = column_ref[0] == row_ref[0, :, some]
            masked = masked_scores(key, joint_ref[0, here, some], bias_ref[head, :, some], same)
            peak = jnp.max(masked, axis=0, keepdims=True)
            unscaled = jnp.exp(masked - peak)
            total = jnp.sum(unscaled, axis=0, keepdims=True)
            weight_low = (unscaled * (1.0 / total)).astype(low)
            log_ref[0, pl.ds(head, 1), some] = peak + jnp.log(total)
            attended_ref[0, here, some] = dot(value, weight_low).astype(low)
    partial = contract_first(attended_ref[0], w_ref[pl.ds(3 * width, width)])
    if last:
        part_rows(core_ref, partial + given_ref[...], per, keep_ref, send_ref)
    else:
        partial_ref[...] = partial


def row_pieces(mine, other, length):
    rows, width = mine.shape
    half = math.gcd(rows, length)
    per = rows // half
    parts = length // half
    operands = []
    specs = []
    for part in range(parts):
        spec = pl.BlockSpec((half, width), lambda i, part=part: ((i * parts + part) % per, 0))
        operands += [mine, other]
        specs += [spec, spec]
    return operands, specs, per, parts


def attend(core, mine, other, segments, w_attn, base, given):
    seq_count, length = segments.shape
    rows, width = mine.shape
    total = seq_count * length
    joint_width = w_attn.shape[0] * 3 // 4
    head_width = joint_width // 3
    heads = head_width // HEAD_DIM
    chunk = min(length, 256)
    last = given is not None
    f32, low = jnp.float32, jnp.bfloat16
    fixed = lambda *shape: pl.BlockSpec(shape, lambda i: (0,) * len(shape))
    each = lambda *shape: pl.BlockSpec((1,) + shape, lambda i: (i, 0, 0))
    whole = pl.BlockSpec((length, width), lambda i: (i, 0))
    operands, specs, per, parts = row_pieces(mine, other, length)
    operands = [core] + operands + [w_attn, base, segments[:, None, :], segments[:, :, None]]
    specs = (
        [pl.BlockSpec(memory_space=pltpu.SMEM)]
        + specs
        + [
            fixed(joint_width + head_width, width),
            fixed(heads, 8, base.shape[2]),
            each(1, length),
            each(length, 1),
        ]
    )
    if last:
        operands.append(given)
        specs.append(whole)
        out_specs = [fixed(rows, width), fixed(rows, width)]
        out_shape = [
            jax.ShapeDtypeStruct((rows, width), f32),
            jax.ShapeDtypeStruct((rows, width), low),
        ]
    else:
        out_specs = [whole]
        out_shape = [jax.ShapeDtypeStruct((total, width), f32)]
    pairs = seq_count * heads * length * length
    return pl.pallas_call(
        functools.partial(attend_kernel, heads, chunk, per, parts, last),
        grid=(seq_count,),
        in_specs=specs,
        out_specs=[each(joint_width, length), each(head_width, length), each(8, length)]
        + out_specs,
        out_shape=[
            jax.ShapeDtypeStruct((seq_count, joint_width, length), low),
            jax.ShapeDtypeStruct((seq_count, head_width, length), low),
            jax.ShapeDtypeStruct((seq_count, 8, length), f32),
        ]
        + out_shape,
        scratch_shapes=[
            pltpu.VMEM((heads, length, length), f32),
            pltpu.VMEM((length, width), low),
        ],
        compiler_params=pltpu.CompilerParams(vmem_limit_bytes=48 * 1024 * 1024),
        cost_estimate=pl.CostEstimate(
            flops=pairs * HEAD_DIM * 16 + total * width * head_width * 8,
            bytes_accessed=total * width * 8 + joint_width * width * 4,
            transcendentals=pairs,
        ),
        name="attend",
    )(*operands)


def attend_back_kernel(heads, chunk, per, parts, last, core_ref, *refs):
    x_pieces, refs = refs[: 2 * parts], refs[2 * parts :]
    g_pieces, refs = refs[: 2 * parts], refs[2 * parts :]
    w_ref, base_ref, row_ref, column_ref, joint_ref, attended_ref, log_ref, *refs = refs
    if last:
        given_ref, w_grad_ref, table_ref, keep_ref, send_ref, *refs = refs
    else:
        w_grad_ref, table_ref, normed_ref, *refs = refs
    bias_ref, total_ref, back_ref, grad_ref, sum_ref, x_ref, g_ref = refs
    low = jnp.bfloat16
    length = x_ref.shape[0]
    width = heads * HEAD_DIM
    span = base_ref.shape[2]
    joint_rows = pl.ds(0, 3 * width)
    out_rows = pl.ds(3 * width, width)

    @pl.when(pl.program_id(0) == 0)
    def _():
        for head in range(heads):
            bias_ref[head] = spread_diagonals(base_ref[head], length)[:, :length]
        total_ref[...] = jnp.zeros_like(total_ref)
        sum_ref[...] = jnp.zeros_like(sum_ref)

    sequence_rows(core_ref, x_pieces, per, x_ref)
    sequence_rows(core_ref, g_pieces, per, g_ref)
    sum_ref[out_rows] += dot(attended_ref[0], g_ref[...])
    back_ref[...] = contract_last(w_ref[out_rows], g_ref[...]).astype(low)
    for head in range(heads):
        first = head * HEAD_DIM
        here = pl.ds(first, HEAD_DIM)
        key = joint_ref[0, pl.ds(width + first, HEAD_DIM)]
        value = joint_ref[0, pl.ds(2 * width + first, HEAD_DIM)]
        grad_key = 0.0
        grad_value = 0.0
        for start in range(0, length, chunk):
            some = pl.ds(start, chunk)
            query = joint_ref[0, here, some]
            back = back_ref[here, some]
            same = column_ref[0] == row_ref[0, :, some]
            masked = masked_scores(key, query, bias_ref[head, :, some], same)
            weight = jnp.exp(masked - log_ref[0, pl.ds(head, 1), some])
            grad_weight = contract_first(value, back)
            grad_value = grad_value + contract_last(back, weight.astype(low))
            delta = jnp.sum(weight * grad_weight, axis=0, keepdims=True)
            grad_scores = (weight * (grad_weight - delta)).astype(low)
            total_ref[head, :, some] += grad_scores.astype(jnp.float32)
            grad_key = grad_key + contract_last(query, grad_scores)
            grad_ref[here, some] = dot(key, grad_scores).astype(low)
        grad_ref[pl.ds(width + first, HEAD_DIM), :] = grad_key.astype(low)
        grad_ref[pl.ds(2 * width + first, HEAD_DIM), :] = grad_value.astype(low)
    sum_ref[joint_rows] += dot(grad_ref[...], x_ref[...])
    normed = contract_first(grad_ref[...], w_ref[joint_rows])
    if last:
        part_rows(core_ref, normed + given_ref[...], per, keep_ref, send_ref)
    else:
        normed_ref[...] = normed

    @pl.when(pl.program_id(0) == pl.num_programs(0) - 1)
    def _():
        w_grad_ref[...] = sum_ref[...].astype(w_grad_ref.dtype)
        for head in range(heads):
            padded = jnp.concatenate(
                [total_ref[head], jnp.zeros((length, span - length), jnp.float32)], axis=1
            )
            table_ref[head] = fold_diagonals(padded, length)


def attend_back(core, kept, mine, other, grad_mine, grad_other, segments, w_attn, base, given):
    joint, attended, logs = kept
    seq_count, length = segments.shape
    rows, width = mine.shape
    total = seq_count * length
    attn_rows = w_attn.shape[0]
    joint_width = attn_rows * 3 // 4
    head_width = joint_width // 3
    heads = head_width // HEAD_DIM
    chunk = min(length, 256)
    last = given is not None
    f32, low = jnp.float32, jnp.bfloat16
    fixed = lambda *shape: pl.BlockSpec(shape, lambda i: (0,) * len(shape))
    each = lambda *shape: pl.BlockSpec((1,) + shape, lambda i: (i, 0, 0))
    whole = pl.BlockSpec((length, width), lambda i: (i, 0))
    operands, specs, per, parts = row_pieces(mine, other, length)
    grad_operands, grad_specs, _, _ = row_pieces(grad_mine, grad_other, length)
    operands = (
        [core]
        + operands
        + grad_operands
        + [w_attn, base, segments[:, None, :], segments[:, :, None], joint, attended, logs]
    )
    specs = (
        [pl.BlockSpec(memory_space=pltpu.SMEM)]
        + specs
        + grad_specs
        + [
            fixed(attn_rows, width),
            fixed(heads, 8, base.shape[2]),
            each(1, length),
            each(length, 1),
            each(joint_width, length),
            each(head_width, length),
            each(8, length),
        ]
    )
    if last:
        operands.append(given)
        specs.append(whole)
        out_specs = [fixed(rows, width), fixed(rows, width)]
        out_shape = [
            jax.ShapeDtypeStruct((rows, width), f32),
            jax.ShapeDtypeStruct((rows, width), low),
        ]
    else:
        out_specs = [whole]
        out_shape = [jax.ShapeDtypeStruct((total, width), f32)]
    pairs = seq_count * heads * length * length
    return pl.pallas_call(
        functools.partial(attend_back_kernel, heads, chunk, per, parts, last),
        grid=(seq_count,),
        in_specs=specs,
        out_specs=[fixed(attn_rows, width), fixed(heads, 8, base.shape[2])] + out_specs,
        out_shape=[
            jax.ShapeDtypeStruct((attn_rows, width), f32 if last else low),
            jax.ShapeDtypeStruct((heads, 8, base.shape[2]), f32),
        ]
        + out_shape,
        scratch_shapes=[
            pltpu.VMEM((heads, length, length), f32),
            pltpu.VMEM((heads, length, length), f32),
            pltpu.VMEM((head_width, length), low),
            pltpu.VMEM((joint_width, length), low),
            pltpu.VMEM((attn_rows, width), f32),
            pltpu.VMEM((length, width), low),
            pltpu.VMEM((length, width), low),
        ],
        compiler_params=pltpu.CompilerParams(vmem_limit_bytes=56 * 1024 * 1024),
        cost_estimate=pl.CostEstimate(
            flops=pairs * HEAD_DIM * 40 + total * width * head_width * 16,
            bytes_accessed=total * width * 16 + joint_width * width * 8,
            transcendentals=pairs,
        ),
        name="attend_back",
    )(*operands)


def bias_base(table, length):
    span = 2 * length
    offset = jnp.arange(span, dtype=jnp.int32)[None, :] - jnp.arange(8, dtype=jnp.int32)[:, None]
    offset = jnp.where(offset < 0, offset + span, offset)
    relative = jnp.where(offset < length, -offset, span - offset)
    onehot = bucket_onehot(relative, table.shape[0])
    return jnp.einsum("stb,bh->hst", onehot, table, precision=lax.Precision.HIGHEST)


def table_grad(folded, table_rows, length):
    span = 2 * length
    offset = jnp.arange(span, dtype=jnp.int32)[None, :] - jnp.arange(8, dtype=jnp.int32)[:, None]
    offset = jnp.where(offset < 0, offset + span, offset)
    relative = jnp.where(offset < length, -offset, span - offset)
    onehot = bucket_onehot(relative, table_rows)
    return jnp.einsum("stb,hst->bh", onehot, folded, precision=lax.Precision.HIGHEST)


def local(
    sizes,
    tokens,
    segments,
    routes,
    attn_gain,
    w_query,
    w_key,
    w_value,
    w_output,
    bias_table,
    ffn_gain,
    w_router,
    expert_in,
    expert_out,
    cotangent,
):
    n_exp, n_tp = sizes
    rows, width = tokens.shape
    group_seqs, length = segments.shape
    head_width = w_query.shape[1]
    experts = w_router.shape[1]
    capacity = rows * 5 // (4 * experts)
    low = jnp.bfloat16
    my_exp = lax.axis_index("exp")
    my_tp = lax.axis_index("tp")
    my_core = my_tp % 2
    pair_seqs = group_seqs * 2 // n_tp
    seqs = lax.dynamic_slice_in_dim(segments, (my_tp // 2) * pair_seqs, pair_seqs, 0)

    core = my_core.astype(jnp.int32)[None]

    joint_width = 3 * head_width
    w_attn = jnp.concatenate([w_query.T, w_key.T, w_value.T, w_output], axis=0)
    w_attn_far = swap(w_attn, "tp", n_tp, 2)
    table_far = swap(bias_table, "tp", n_tp, 2)
    expert_both = jnp.concatenate([expert_in[0], expert_out[0]], axis=0)
    w_attn_far, expert_both = ordered(w_attn_far, expert_both)

    place = jnp.arange(rows, dtype=jnp.int32)
    choose = routes[:, None] == jnp.arange(experts, dtype=jnp.int32)[None, :]
    choose_float = choose.astype(jnp.float32)
    rank = dot((place[:, None] > place[None, :]).astype(low), choose.astype(low))
    slot = jnp.sum(rank * choose_float, axis=-1).astype(jnp.int32)
    target = jnp.where(slot < capacity, (routes ^ my_exp) * capacity + slot, experts * capacity)
    spread = (
        target[None, :] == jnp.arange(experts * capacity, dtype=jnp.int32)[:, None]
    ).astype(low)

    def pack(data):
        return dot(spread, data).astype(low).reshape(experts, capacity, width)

    def unpack(data):
        return contract_first(spread, data)

    packed_cotangent = pack(cotangent)
    cotangent_first = first_wave(packed_cotangent, "exp", n_exp, (4, 5, 6))

    inputs = tokens.astype(jnp.float32)
    scale_one = rms_scale(inputs)
    normed_low = (inputs * scale_one * attn_gain).astype(low)
    normed_other = swap(normed_low, "tp", n_tp, 1)
    base = bias_base(bias_table, length)
    *kept, partial = attend(core, normed_low, normed_other, seqs, w_attn, base, None)
    partial, (packed_cotangent, table_far) = ordered(partial, (packed_cotangent, table_far))
    base_far = bias_base(table_far, length)
    cotangent_first, partial = ordered(cotangent_first, partial)
    cotangent_next = next_wave(packed_cotangent, "exp", n_exp, (7, 1, 2, 3))

    expert_far = swap(expert_both, "tp", n_tp, 2)

    *kept_far, keep, send = attend(
        core, normed_low, normed_other, seqs, w_attn_far, base_far, partial
    )
    cotangent_next, send = ordered(cotangent_next, send)
    residual = inputs + (keep + swap(send, "tp", n_tp, 1).astype(jnp.float32))

    scale_two = rms_scale(residual)
    mixed_low = (residual * scale_two * ffn_gain).astype(low)
    router_share = jax.nn.softmax(dot(mixed_low, w_router), axis=-1)
    gate = jnp.sum(router_share * choose_float, axis=-1)
    cotangent_sent = join(packed_cotangent, cotangent_first, cotangent_next)
    cotangent_sent, packed = ordered(cotangent_sent, pack(mixed_low))
    first = first_wave(packed, "exp", n_exp, (4, 5, 1, 2))
    early = chosen(first, (4, 5, 1, 2))
    early, (packed, expert_both, expert_far) = ordered(early, (packed, expert_both, expert_far))
    first.update(early)
    then = next_wave(packed, "exp", n_exp, (6, 7, 3))
    expert_near = swap(expert_both, "tp", n_tp, 1)
    expert_all = [expert_both, expert_near, expert_far, swap(expert_far, "tp", n_tp, 1)]
    received = join(packed, first, then).reshape(-1, width)

    produced_low, grad_sent, grad_rows, gate_grad_rows, active, grad_upper = expert_pass(
        received, cotangent_sent.reshape(-1, width), w_router, my_exp, expert_all
    )

    def thirds(value):
        first = value.astype(low)
        rest = value - first.astype(jnp.float32)
        second = rest.astype(low)
        third = (rest - second.astype(jnp.float32)).astype(low)
        return jnp.stack([first, second, third], axis=1)

    extra = thirds(gate_grad_rows.reshape(experts, capacity))
    extra = jnp.pad(extra, ((0, 0), (0, 0), (0, width // 3 - capacity))).reshape(experts, 1, width)
    grad_block = jnp.concatenate(
        [grad_sent.reshape(experts, capacity, width), extra], axis=1
    )
    first = first_wave(grad_block, "exp", n_exp, (4, 5, 1, 2, 3))
    pieces = (received, grad_upper, active, grad_rows)
    first[1], pieces = ordered(first[1], pieces)

    outer_send = expert_outer(*pieces, 1, low)
    early = chosen(first, (4, 1, 2, 3))
    (outer_send, early), (pieces, grad_block) = ordered((outer_send, early), (pieces, grad_block))
    first.update(early)
    then = next_wave(grad_block, "exp", n_exp, (6, 7))
    outer_given = swap(outer_send, "tp", n_tp, 1)
    outer_keep = expert_outer(*pieces, 0, low)
    outer_keep, (first, then) = ordered(outer_keep, (first, then))
    grad_block = join(grad_block, first, then)
    grad_back = unpack(grad_block[:, :capacity].reshape(-1, width))
    gate_parts = grad_block[:, capacity].reshape(experts, 3, width // 3)[:, :, :capacity]
    gate_flat = jnp.sum(gate_parts.astype(jnp.float32), axis=1).reshape(-1)
    gate_grad = jnp.sum(spread.astype(jnp.float32) * gate_flat[:, None], axis=0)

    upstream = cotangent.astype(jnp.float32)
    logit_grad = ((gate_grad * gate)[:, None] * (choose_float - router_share)).astype(low)
    grad_router = contract_first(mixed_low, logit_grad)
    grad_mixed = contract_last(logit_grad, w_router) + grad_back
    normal = residual * scale_two
    scaled = grad_mixed * ffn_gain
    grad_ffn_gain = jnp.sum(grad_mixed * normal, axis=0)
    grad_residual = upstream + scale_two * (
        scaled - normal * jnp.mean(scaled * normal, axis=-1, keepdims=True)
    )
    grad_low = grad_residual.astype(low)
    grad_other = swap(grad_low, "tp", n_tp, 1)

    outer_given, grad_other = ordered(outer_given, grad_other)

    def added(place, some):
        return outer_keep[place, some].astype(jnp.float32) + outer_given[place, some].astype(
            jnp.float32
        )

    across_in = swap(added(1, slice(0, width)).astype(low), "tp", n_tp, 2)
    grad_other, produced_low = ordered(grad_other, produced_low)
    produced_low = produced_low.reshape(experts, capacity, width)
    first = first_wave(produced_low, "exp", n_exp, (4, 5, 6, 7))

    grad_attn_far, folded_far, grad_normed = attend_back(
        core, kept_far, normed_low, normed_other, grad_low, grad_other, seqs, w_attn_far, base_far, None
    )
    (first, across_in, grad_attn_far), (folded_far, grad_normed, produced_low) = ordered(
        (first, across_in, grad_attn_far), (folded_far, grad_normed, produced_low)
    )
    then = next_wave(produced_low, "exp", n_exp, (1, 2, 3))
    grad_attn_far = swap(grad_attn_far, "tp", n_tp, 2)
    table_rows = bias_table.shape[0]
    table_far = swap(table_grad(folded_far, table_rows, length), "tp", n_tp, 2)
    grad_attn, folded, keep, send = attend_back(
        core, kept, normed_low, normed_other, grad_low, grad_other, seqs, w_attn, base, grad_normed
    )
    (then, grad_attn_far), (send, grad_attn) = ordered((then, grad_attn_far), (send, grad_attn))
    grad_normed = keep + swap(send, "tp", n_tp, 1).astype(jnp.float32)
    normal = inputs * scale_one
    scaled = grad_normed * attn_gain
    grad_attn_gain = jnp.sum(grad_normed * normal, axis=0)
    grad_tokens = grad_residual + scale_one * (
        scaled - normal * jnp.mean(scaled * normal, axis=-1, keepdims=True)
    )
    grad_table = table_grad(folded, table_rows, length) + table_far
    grad_attn = grad_attn + grad_attn_far.astype(jnp.float32)
    small = jnp.concatenate(
        [grad_attn_gain, grad_ffn_gain, grad_router.T.reshape(-1), grad_table.reshape(-1)]
    )
    small_size = (2 + experts) * width

    bits = [1 << place for place in range(n_exp.bit_length() - 1)]
    turned = bits[1:] + bits[:1]
    middle = grad_attn.shape[0] // 2
    wide = [grad_attn[:middle], grad_attn[middle:]]
    steps = [(halve, first_bit, second_bit) for first_bit, second_bit in zip(bits, turned)]
    steps += [(double, second, first_) for first_, second in zip(turned[::-1], bits[::-1])]
    small_steps = [None] + [("exp", n_exp, bit) for bit in bits]
    small_steps += [("tp", n_tp, 1 << place) for place in range(n_tp.bit_length() - 1)]
    small_steps += [None] * (len(steps) - len(small_steps))
    late = (first, then, outer_keep, outer_given)
    for place, (step, *both_bits) in enumerate(steps):
        if step is double and place == len(bits):
            wide = [value.astype(low) for value in wide]
        if place == len(steps) - 2:
            wide, (across_in, across_out) = ordered(wide, (across_in, across_out))
            across_out, wide = ordered(across_out, wide)
        wide = [step(value, "exp", n_exp, bit) for value, bit in zip(wide, both_bits)]
        if small_steps[place] is not None:
            axis, size, bit = small_steps[place]
            if axis == "tp" and bit == 1:
                grad_table = small[small_size:].reshape(grad_table.shape)
                small = small[:small_size]
            small = small + swap(small, axis, size, bit)
            wide, small = lax.optimization_barrier((wide, small))
        if place == 0:
            wide, late = ordered(wide, late)
            first, then, outer_keep, outer_given = late
            across_out = swap(added(1, slice(width, None)).astype(low), "tp", n_tp, 2)
            returned = unpack(join(produced_low, first, then).reshape(-1, width))
            mixed = (residual + gate[:, None] * returned).astype(low)
    grad_expert_in = (added(0, slice(0, width)) + across_in.astype(jnp.float32))[None]
    grad_expert_out = (added(0, slice(width, None)) + across_out.astype(jnp.float32))[None]
    grad_attn = jnp.concatenate(wide, axis=0).astype(jnp.float32)
    small = small.reshape(-1, width)
    return (
        mixed,
        grad_tokens,
        small[0],
        grad_attn[:head_width].T,
        grad_attn[head_width : 2 * head_width].T,
        grad_attn[2 * head_width : joint_width].T,
        grad_attn[joint_width:],
        grad_table,
        small[1],
        small[2:].T,
        grad_expert_in,
        grad_expert_out,
    )


def solution(mesh):
    placed = (
        P(("exp", "tp"), None),
        P("exp", None),
        P(("exp", "tp")),
        P(),
        P(None, "tp"),
        P(None, "tp"),
        P(None, "tp"),
        P("tp", None),
        P(None, "tp"),
        P(),
        P(),
        P("exp", None, "tp"),
        P("exp", "tp", None),
        P(("exp", "tp"), None),
    )
    return jax.shard_map(
        functools.partial(local, (mesh.shape["exp"], mesh.shape["tp"])),
        mesh=mesh,
        in_specs=placed,
        out_specs=(
            P(("exp", "tp"), None),
            P(("exp", "tp"), None),
            P(),
            P(None, "tp"),
            P(None, "tp"),
            P(None, "tp"),
            P("tp", None),
            P(None, "tp"),
            P(),
            P(),
            P("exp", None, "tp"),
            P("exp", "tp", None),
        ),
        check_vma=False,
    )
```

```python
import functools
import math

import jax
import jax.numpy as jnp
from jax import lax
from jax.experimental import pallas as pl
from jax.experimental.pallas import tpu as pltpu
from jax.sharding import PartitionSpec as P

HEAD_DIM = 64


EPSILON = 1e-06
MASKED_SCORE = -1000000000.0
thresholds = (8, 12, 16, 23, 32, 46, 64, 91)


def bucket_of(relative):
    distance = jnp.abs(relative)
    distant = 7 + sum(((distance >= boundary).astype(jnp.int32) for boundary in thresholds))
    return jnp.where(distance < 8, distance, distant) + jnp.where(relative > 0, 16, 0)


def bucket_onehot(relative, table_rows):
    return (
        bucket_of(relative)[..., None] == jnp.arange(table_rows, dtype=jnp.int32)
    ).astype(jnp.float32)


def rms_scale(values):
    return lax.rsqrt(jnp.mean(values * values, axis=-1, keepdims=True) + EPSILON)


def dot(left, right):
    return jnp.dot(left, right, preferred_element_type=jnp.float32)


def contract_first(left, right):
    return lax.dot_general(
        left, right, (((0,), (0,)), ((), ())), preferred_element_type=jnp.float32
    )


def contract_last(left, right):
    return lax.dot_general(
        left, right, (((1,), (1,)), ((), ())), preferred_element_type=jnp.float32
    )


def gelu_both(upper):
    slope = 0.7978845608028654
    square = upper * upper
    bend = jnp.tanh(slope * upper * (1.0 + 0.044715 * square))
    half = 0.5 * (1.0 + bend)
    active = upper * half
    derivative = half + 0.5 * upper * (1.0 - bend * bend) * slope * (1.0 + 3 * 0.044715 * square)
    return active, derivative


def swap(value, axis, size, bit):
    return lax.ppermute(value, axis, [(place, place ^ bit) for place in range(size)])


def trade_all(blocks, axis, size):
    stride = 1
    while stride < size:
        digit = min(8, size // stride)
        shape = blocks.shape
        view = blocks.reshape((size // (stride * digit), digit, stride) + shape[1:])
        parts = [view[:, 0]]
        for step in range(1, digit):
            parts.append(swap(view[:, step], axis, size, step * stride))
        blocks = jnp.stack(parts, axis=1).reshape(shape)
        stride *= digit
    return blocks


def first_wave(blocks, axis, size, steps):
    if size > 8:
        whole = trade_all(blocks, axis, size)
        return {step: whole[step] for step in range(1, size)}
    return {step: swap(blocks[step], axis, size, step) for step in steps if step < size}


def next_wave(blocks, axis, size, steps):
    if size > 8:
        return {}
    return {step: swap(blocks[step], axis, size, step) for step in steps if step < size}


def join(blocks, *waves):
    got = {0: blocks[0]}
    for wave in waves:
        got.update(wave)
    return jnp.stack([got[step] for step in range(blocks.shape[0])])


def chosen(wave, steps):
    return {step: wave[step] for step in steps if step in wave}


def ordered(earlier, later):
    return lax.optimization_barrier((earlier, later))


def halve(value, axis, size, bit):
    side = (lax.axis_index(axis) // bit) % 2
    half = value.shape[0] // 2
    keep = lax.dynamic_slice_in_dim(value, side * half, half, 0)
    send = lax.dynamic_slice_in_dim(value, (1 - side) * half, half, 0)
    return keep + swap(send.astype(jnp.bfloat16), axis, size, bit).astype(jnp.float32)


def double(value, axis, size, bit):
    other = swap(value, axis, size, bit)
    return jnp.where(
        (lax.axis_index(axis) // bit) % 2 == 0,
        jnp.concatenate([value, other], axis=0),
        jnp.concatenate([other, value], axis=0),
    )


def spread_diagonals(block, rows):
    held = block.shape[0]
    while held < rows:
        block = jnp.concatenate([block, pltpu.roll(block, held, 1)], axis=0)
        held *= 2
    return block


def fold_diagonals(block, rows):
    span = block.shape[1]
    while rows > 8:
        rows //= 2
        block = block[:rows] + pltpu.roll(block[rows:], span - rows, 1)
    return block


def masked_scores(key, query, bias, same):
    scores = contract_first(key, query) + bias
    return jnp.where(same, scores, MASKED_SCORE)


def expert_kernel(
    x_ref,
    g_ref,
    router_ref,
    mine_ref,
    *refs,
):
    weights = refs[:8]
    (
        produced_ref,
        sent_ref,
        grad_rows_ref,
        gate_ref,
        active_ref,
        upper_ref,
        held_ref,
        semaphores,
    ) = refs[8:]
    low = jnp.bfloat16
    width = x_ref.shape[1]
    first = pl.program_id(0) == 0
    copies = [
        pltpu.make_async_copy(weight, held_ref.at[place], semaphores.at[place])
        for place, weight in enumerate(weights)
    ]

    @pl.when(first)
    def _():
        for copy in copies:
            copy.start()

    logits = dot(x_ref[...], router_ref[...])
    logits = logits - jnp.max(logits, axis=1, keepdims=True)
    unscaled = jnp.exp(logits)
    gate = jnp.sum(unscaled * mine_ref[...], axis=1, keepdims=True) / jnp.sum(
        unscaled, axis=1, keepdims=True
    )
    grad_rows = (gate * g_ref[...].astype(jnp.float32)).astype(low)
    grad_rows_ref[...] = grad_rows
    produced = jnp.zeros(x_ref.shape, jnp.float32)
    sent = jnp.zeros(x_ref.shape, jnp.float32)
    for place in range(len(weights) // 2):

        @pl.when(first)
        def _():
            copies[2 * place].wait()
            copies[2 * place + 1].wait()

        weight_in = held_ref[2 * place]
        weight_out = held_ref[2 * place + 1]
        columns = pl.ds(place * width, width)
        active, derivative = gelu_both(dot(x_ref[...], weight_in))
        active = active.astype(low)
        upper = (contract_last(grad_rows, weight_out) * derivative).astype(low)
        active_ref[:, columns] = active
        upper_ref[:, columns] = upper
        produced = produced + dot(active, weight_out)
        sent = sent + contract_last(upper, weight_in)
    produced = produced.astype(low)
    produced_ref[...] = produced
    sent_ref[...] = sent.astype(low)
    gate_ref[...] = jnp.sum(
        g_ref[...].astype(jnp.float32) * produced.astype(jnp.float32), axis=1, keepdims=True
    )


def expert_pass(received, cotangent_rows, w_router, my_expert, weights):
    rows, width = received.shape
    experts = w_router.shape[1]
    tile = 240
    hidden = width * len(weights) // 2
    low = jnp.bfloat16
    is_mine = (jnp.arange(experts, dtype=jnp.int32) == my_expert).astype(jnp.float32)[None, :]
    tiled = lambda columns: pl.BlockSpec((tile, columns), lambda i: (i, 0))
    fixed = lambda *shape: pl.BlockSpec(shape, lambda i: (0,) * len(shape))
    shape = lambda columns, dtype: jax.ShapeDtypeStruct((rows, columns), dtype)
    return pl.pallas_call(
        expert_kernel,
        grid=(rows // tile,),
        in_specs=[tiled(width), tiled(width), fixed(width, experts), fixed(1, experts)]
        + [pl.BlockSpec(memory_space=pl.ANY)] * len(weights),
        out_specs=[
            tiled(width),
            tiled(width),
            tiled(width),
            tiled(1),
            tiled(hidden),
            tiled(hidden),
        ],
        out_shape=[
            shape(width, low),
            shape(width, low),
            shape(width, low),
            shape(1, jnp.float32),
            shape(hidden, low),
            shape(hidden, low),
        ],
        scratch_shapes=[
            pltpu.VMEM((len(weights), width, width), low),
            pltpu.SemaphoreType.DMA((len(weights),)),
        ],
        compiler_params=pltpu.CompilerParams(vmem_limit_bytes=48 * 1024 * 1024),
        cost_estimate=pl.CostEstimate(
            flops=rows * width * hidden * 8,
            bytes_accessed=rows * hidden * 4 + width * hidden * 4,
            transcendentals=rows * hidden,
        ),
        name="expert_pass",
    )(received, cotangent_rows, w_router, is_mine, *weights)


def outer_kernel(x_ref, upper_ref, active_ref, grad_ref, out_ref):
    width = x_ref.shape[1]
    out_ref[0, pl.ds(0, width)] = contract_first(x_ref[...], upper_ref[...]).astype(out_ref.dtype)
    out_ref[0, pl.ds(width, width)] = contract_first(active_ref[...], grad_ref[...]).astype(
        out_ref.dtype
    )


def expert_outer(received, grad_upper, active, grad_rows, first, dtype):
    rows, width = received.shape
    count = active.shape[1] // width // 2
    fixed = pl.BlockSpec((rows, width), lambda i: (0, 0))
    some = pl.BlockSpec((rows, width), lambda i: (0, 2 * i + first))
    return pl.pallas_call(
        outer_kernel,
        grid=(count,),
        in_specs=[fixed, some, some, fixed],
        out_specs=pl.BlockSpec((1, 2 * width, width), lambda i: (i, 0, 0)),
        out_shape=jax.ShapeDtypeStruct((count, 2 * width, width), dtype),
        compiler_params=pltpu.CompilerParams(vmem_limit_bytes=48 * 1024 * 1024),
        cost_estimate=pl.CostEstimate(
            flops=rows * width * width * 4 * count,
            bytes_accessed=rows * width * 8 + count * width * width * 8,
            transcendentals=0,
        ),
        name="expert_outer",
    )(received, grad_upper, active, grad_rows)


def sequence_rows(core_ref, pieces, per, held_ref):
    half = pieces[0].shape[0]
    for part in range(len(pieces) // 2):
        place = pl.program_id(0) * (len(pieces) // 2) + part
        is_mine = (place >= per) == (core_ref[0] == 1)

        @pl.when(is_mine)
        def _():
            held_ref[pl.ds(part * half, half)] = pieces[2 * part][...]

        @pl.when(jnp.logical_not(is_mine))
        def _():
            held_ref[pl.ds(part * half, half)] = pieces[2 * part + 1][...]


def part_rows(core_ref, value, per, keep_ref, send_ref):
    half = keep_ref.shape[0] // per
    count = value.shape[0] // half
    for part in range(count):
        place = pl.program_id(0) * count + part
        is_mine = (place >= per) == (core_ref[0] == 1)
        here = pl.ds(pl.multiple_of((place % per) * half, half), half)
        some = value[part * half : (part + 1) * half]

        @pl.when(is_mine)
        def _():
            keep_ref[here] = some

        @pl.when(jnp.logical_not(is_mine))
        def _():
            send_ref[here] = some.astype(send_ref.dtype)


def attend_kernel(heads, chunk, per, parts, last, core_ref, *refs):
    pieces, refs = refs[: 2 * parts], refs[2 * parts :]
    w_ref, base_ref, row_ref, column_ref, *refs = refs
    if last:
        given_ref, joint_ref, attended_ref, log_ref, keep_ref, send_ref, bias_ref, x_ref = refs
    else:
        joint_ref, attended_ref, log_ref, partial_ref, bias_ref, x_ref = refs
    low = jnp.bfloat16
    length = x_ref.shape[0]
    width = heads * HEAD_DIM

    @pl.when(pl.program_id(0) == 0)
    def _():
        for head in range(heads):
            bias_ref[head] = spread_diagonals(base_ref[head], length)[:, :length]

    sequence_rows(core_ref, pieces, per, x_ref)
    joint_ref[0] = contract_last(w_ref[pl.ds(0, 3 * width)], x_ref[...]).astype(low)
    work = [(head, start) for head in range(heads) for start in range(0, length, chunk)]

    def score(head, start):
        first = head * HEAD_DIM
        some = pl.ds(start, chunk)
        same = column_ref[0] == row_ref[0, :, some]
        key = joint_ref[0, pl.ds(width + first, HEAD_DIM)]
        query = joint_ref[0, pl.ds(first, HEAD_DIM), some]
        return masked_scores(key, query, bias_ref[head, :, some], same)

    ahead = score(*work[0])
    for place, (head, start) in enumerate(work):
        masked = ahead
        if place + 1 < len(work):
            ahead = score(*work[place + 1])
        first = head * HEAD_DIM
        some = pl.ds(start, chunk)
        peak = jnp.max(masked, axis=0, keepdims=True)
        unscaled = jnp.exp(masked - peak)
        total = jnp.sum(unscaled, axis=0, keepdims=True)
        weight_low = (unscaled * (1.0 / total)).astype(low)
        log_ref[0, pl.ds(head, 1), some] = peak + jnp.log(total)
        value = joint_ref[0, pl.ds(2 * width + first, HEAD_DIM)]
        attended_ref[0, pl.ds(first, HEAD_DIM), some] = dot(value, weight_low).astype(low)
    partial = contract_first(attended_ref[0], w_ref[pl.ds(3 * width, width)])
    if last:
        part_rows(core_ref, partial + given_ref[...], per, keep_ref, send_ref)
    else:
        partial_ref[...] = partial


def row_pieces(mine, other, length):
    rows, width = mine.shape
    half = math.gcd(rows, length)
    per = rows // half
    parts = length // half
    operands = []
    specs = []
    for part in range(parts):
        spec = pl.BlockSpec((half, width), lambda i, part=part: ((i * parts + part) % per, 0))
        operands += [mine, other]
        specs += [spec, spec]
    return operands, specs, per, parts


def attend(core, mine, other, segments, w_attn, base, given):
    seq_count, length = segments.shape
    rows, width = mine.shape
    total = seq_count * length
    joint_width = w_attn.shape[0] * 3 // 4
    head_width = joint_width // 3
    heads = head_width // HEAD_DIM
    chunk = min(length, 512)
    last = given is not None
    f32, low = jnp.float32, jnp.bfloat16
    fixed = lambda *shape: pl.BlockSpec(shape, lambda i: (0,) * len(shape))
    each = lambda *shape: pl.BlockSpec((1,) + shape, lambda i: (i, 0, 0))
    whole = pl.BlockSpec((length, width), lambda i: (i, 0))
    operands, specs, per, parts = row_pieces(mine, other, length)
    operands = [core] + operands + [w_attn, base, segments[:, None, :], segments[:, :, None]]
    specs = (
        [pl.BlockSpec(memory_space=pltpu.SMEM)]
        + specs
        + [
            fixed(joint_width + head_width, width),
            fixed(heads, 8, base.shape[2]),
            each(1, length),
            each(length, 1),
        ]
    )
    if last:
        operands.append(given)
        specs.append(whole)
        out_specs = [fixed(rows, width), fixed(rows, width)]
        out_shape = [
            jax.ShapeDtypeStruct((rows, width), f32),
            jax.ShapeDtypeStruct((rows, width), low),
        ]
    else:
        out_specs = [whole]
        out_shape = [jax.ShapeDtypeStruct((total, width), f32)]
    pairs = seq_count * heads * length * length
    return pl.pallas_call(
        functools.partial(attend_kernel, heads, chunk, per, parts, last),
        grid=(seq_count,),
        in_specs=specs,
        out_specs=[each(joint_width, length), each(head_width, length), each(8, length)]
        + out_specs,
        out_shape=[
            jax.ShapeDtypeStruct((seq_count, joint_width, length), low),
            jax.ShapeDtypeStruct((seq_count, head_width, length), low),
            jax.ShapeDtypeStruct((seq_count, 8, length), f32),
        ]
        + out_shape,
        scratch_shapes=[
            pltpu.VMEM((heads, length, length), f32),
            pltpu.VMEM((length, width), low),
        ],
        compiler_params=pltpu.CompilerParams(vmem_limit_bytes=28 * 1024 * 1024),
        cost_estimate=pl.CostEstimate(flops=1 << 20, bytes_accessed=1 << 16, transcendentals=0),
        name="attend",
    )(*operands)


def attend_back_kernel(heads, chunk, per, parts, last, core_ref, *refs):
    x_pieces, refs = refs[: 2 * parts], refs[2 * parts :]
    g_pieces, refs = refs[: 2 * parts], refs[2 * parts :]
    w_ref, base_ref, row_ref, column_ref, joint_ref, attended_ref, log_ref, *refs = refs
    if last:
        given_ref, w_grad_ref, table_ref, keep_ref, send_ref, *refs = refs
    else:
        w_grad_ref, table_ref, normed_ref, *refs = refs
    bias_ref, total_ref, back_ref, grad_ref, sum_ref, x_ref, g_ref = refs
    low = jnp.bfloat16
    length = x_ref.shape[0]
    width = heads * HEAD_DIM
    span = base_ref.shape[2]
    joint_rows = pl.ds(0, 3 * width)
    out_rows = pl.ds(3 * width, width)

    @pl.when(pl.program_id(0) == 0)
    def _():
        for head in range(heads):
            bias_ref[head] = spread_diagonals(base_ref[head], length)[:, :length]
        total_ref[...] = jnp.zeros_like(total_ref)
        sum_ref[...] = jnp.zeros_like(sum_ref)

    sequence_rows(core_ref, x_pieces, per, x_ref)
    sequence_rows(core_ref, g_pieces, per, g_ref)
    sum_ref[out_rows] += dot(attended_ref[0], g_ref[...])
    back_ref[...] = contract_last(w_ref[out_rows], g_ref[...]).astype(low)
    for head in range(heads):
        first = head * HEAD_DIM
        here = pl.ds(first, HEAD_DIM)
        key = joint_ref[0, pl.ds(width + first, HEAD_DIM)]
        value = joint_ref[0, pl.ds(2 * width + first, HEAD_DIM)]
        grad_key = 0.0
        grad_value = 0.0
        for start in range(0, length, chunk):
            some = pl.ds(start, chunk)
            query = joint_ref[0, here, some]
            back = back_ref[here, some]
            same = column_ref[0] == row_ref[0, :, some]
            masked = masked_scores(key, query, bias_ref[head, :, some], same)
            weight = jnp.exp(masked - log_ref[0, pl.ds(head, 1), some])
            grad_weight = contract_first(value, back)
            grad_value = grad_value + contract_last(back, weight.astype(low))
            delta = jnp.sum(weight * grad_weight, axis=0, keepdims=True)
            grad_scores = (weight * (grad_weight - delta)).astype(low)
            total_ref[head, :, some] += grad_scores.astype(jnp.float32)
            grad_key = grad_key + contract_last(query, grad_scores)
            grad_ref[here, some] = dot(key, grad_scores).astype(low)
        grad_ref[pl.ds(width + first, HEAD_DIM), :] = grad_key.astype(low)
        grad_ref[pl.ds(2 * width + first, HEAD_DIM), :] = grad_value.astype(low)
    sum_ref[joint_rows] += dot(grad_ref[...], x_ref[...])
    normed = contract_first(grad_ref[...], w_ref[joint_rows])
    if last:
        part_rows(core_ref, normed + given_ref[...], per, keep_ref, send_ref)
    else:
        normed_ref[...] = normed

    @pl.when(pl.program_id(0) == pl.num_programs(0) - 1)
    def _():
        w_grad_ref[...] = sum_ref[...].astype(w_grad_ref.dtype)
        for head in range(heads):
            padded = jnp.concatenate(
                [total_ref[head], jnp.zeros((length, span - length), jnp.float32)], axis=1
            )
            table_ref[head] = fold_diagonals(padded, length)


def attend_back(core, kept, mine, other, grad_mine, grad_other, segments, w_attn, base, given):
    joint, attended, logs = kept
    seq_count, length = segments.shape
    rows, width = mine.shape
    total = seq_count * length
    attn_rows = w_attn.shape[0]
    joint_width = attn_rows * 3 // 4
    head_width = joint_width // 3
    heads = head_width // HEAD_DIM
    chunk = min(length, 512)
    last = given is not None
    f32, low = jnp.float32, jnp.bfloat16
    fixed = lambda *shape: pl.BlockSpec(shape, lambda i: (0,) * len(shape))
    each = lambda *shape: pl.BlockSpec((1,) + shape, lambda i: (i, 0, 0))
    whole = pl.BlockSpec((length, width), lambda i: (i, 0))
    operands, specs, per, parts = row_pieces(mine, other, length)
    grad_operands, grad_specs, _, _ = row_pieces(grad_mine, grad_other, length)
    operands = (
        [core]
        + operands
        + grad_operands
        + [w_attn, base, segments[:, None, :], segments[:, :, None], joint, attended, logs]
    )
    specs = (
        [pl.BlockSpec(memory_space=pltpu.SMEM)]
        + specs
        + grad_specs
        + [
            fixed(attn_rows, width),
            fixed(heads, 8, base.shape[2]),
            each(1, length),
            each(length, 1),
            each(joint_width, length),
            each(head_width, length),
            each(8, length),
        ]
    )
    if last:
        operands.append(given)
        specs.append(whole)
        out_specs = [fixed(rows, width), fixed(rows, width)]
        out_shape = [
            jax.ShapeDtypeStruct((rows, width), f32),
            jax.ShapeDtypeStruct((rows, width), low),
        ]
    else:
        out_specs = [whole]
        out_shape = [jax.ShapeDtypeStruct((total, width), f32)]
    pairs = seq_count * heads * length * length
    return pl.pallas_call(
        functools.partial(attend_back_kernel, heads, chunk, per, parts, last),
        grid=(seq_count,),
        in_specs=specs,
        out_specs=[fixed(attn_rows, width), fixed(heads, 8, base.shape[2])] + out_specs,
        out_shape=[
            jax.ShapeDtypeStruct((attn_rows, width), f32 if last else low),
            jax.ShapeDtypeStruct((heads, 8, base.shape[2]), f32),
        ]
        + out_shape,
        scratch_shapes=[
            pltpu.VMEM((heads, length, length), f32),
            pltpu.VMEM((heads, length, length), f32),
            pltpu.VMEM((head_width, length), low),
            pltpu.VMEM((joint_width, length), low),
            pltpu.VMEM((attn_rows, width), f32),
            pltpu.VMEM((length, width), low),
            pltpu.VMEM((length, width), low),
        ],
        compiler_params=pltpu.CompilerParams(vmem_limit_bytes=32 * 1024 * 1024),
        cost_estimate=pl.CostEstimate(
            flops=pairs * HEAD_DIM * 40 + total * width * head_width * 16,
            bytes_accessed=total * width * 16 + joint_width * width * 8,
            transcendentals=pairs,
        ),
        name="attend_back",
    )(*operands)


def bias_base(table, length):
    span = 2 * length
    offset = jnp.arange(span, dtype=jnp.int32)[None, :] - jnp.arange(8, dtype=jnp.int32)[:, None]
    offset = jnp.where(offset < 0, offset + span, offset)
    relative = jnp.where(offset < length, -offset, span - offset)
    onehot = bucket_onehot(relative, table.shape[0])
    return jnp.einsum("stb,bh->hst", onehot, table, precision=lax.Precision.HIGHEST)


def table_grad(folded, table_rows, length):
    span = 2 * length
    offset = jnp.arange(span, dtype=jnp.int32)[None, :] - jnp.arange(8, dtype=jnp.int32)[:, None]
    offset = jnp.where(offset < 0, offset + span, offset)
    relative = jnp.where(offset < length, -offset, span - offset)
    onehot = bucket_onehot(relative, table_rows)
    return jnp.einsum("stb,hst->bh", onehot, folded, precision=lax.Precision.HIGHEST)


def local(
    sizes,
    tokens,
    segments,
    routes,
    attn_gain,
    w_query,
    w_key,
    w_value,
    w_output,
    bias_table,
    ffn_gain,
    w_router,
    expert_in,
    expert_out,
    cotangent,
):
    n_exp, n_tp = sizes
    rows, width = tokens.shape
    group_seqs, length = segments.shape
    head_width = w_query.shape[1]
    experts = w_router.shape[1]
    capacity = rows * 5 // (4 * experts)
    low = jnp.bfloat16
    my_exp = lax.axis_index("exp")
    my_tp = lax.axis_index("tp")
    my_core = my_tp % 2
    pair_seqs = group_seqs * 2 // n_tp
    seqs = lax.dynamic_slice_in_dim(segments, (my_tp // 2) * pair_seqs, pair_seqs, 0)

    core = my_core.astype(jnp.int32)[None]

    joint_width = 3 * head_width
    w_attn = jnp.concatenate([w_query.T, w_key.T, w_value.T, w_output], axis=0)
    table_far = swap(bias_table, "tp", n_tp, 2)
    table_far, w_attn = ordered(table_far, w_attn)
    w_attn_far = swap(w_attn, "tp", n_tp, 2)
    expert_mine = [expert_in[0], expert_out[0]]
    w_attn_far, out_mine = ordered(w_attn_far, expert_mine[1])
    out_far = swap(out_mine, "tp", n_tp, 2)

    place = jnp.arange(rows, dtype=jnp.int32)
    choose = routes[:, None] == jnp.arange(experts, dtype=jnp.int32)[None, :]
    choose_float = choose.astype(jnp.float32)
    rank = dot((place[:, None] > place[None, :]).astype(low), choose.astype(low))
    slot = jnp.sum(rank * choose_float, axis=-1).astype(jnp.int32)
    target = jnp.where(slot < capacity, (routes ^ my_exp) * capacity + slot, experts * capacity)
    spread = (
        target[None, :] == jnp.arange(experts * capacity, dtype=jnp.int32)[:, None]
    ).astype(low)

    def pack(data):
        return dot(spread, data).astype(low).reshape(experts, capacity, width)

    def unpack(data):
        return contract_first(spread, data)

    packed_cotangent = pack(cotangent)
    cotangent_first = first_wave(packed_cotangent, "exp", n_exp, (4, 5, 1))

    inputs = tokens.astype(jnp.float32)
    scale_one = rms_scale(inputs)
    normed_low = (inputs * scale_one * attn_gain).astype(low)
    normed_other = swap(normed_low, "tp", n_tp, 1)
    normed_other, expert_mine = ordered(normed_other, expert_mine)
    in_far = swap(expert_mine[0], "tp", n_tp, 2)
    base = bias_base(bias_table, length)
    *kept, partial = attend(core, normed_low, normed_other, seqs, w_attn, base, None)
    partial, (packed_cotangent, table_far) = ordered(partial, (packed_cotangent, table_far))
    base_far = bias_base(table_far, length)
    cotangent_first, partial = ordered(cotangent_first, partial)
    cotangent_next = next_wave(packed_cotangent, "exp", n_exp, (6, 7, 2, 3))


    *kept_far, keep, send = attend(
        core, normed_low, normed_other, seqs, w_attn_far, base_far, partial
    )
    cotangent_next, (send, expert_mine) = ordered(cotangent_next, (send, expert_mine))
    expert_near = [swap(weights, "tp", n_tp, 1) for weights in expert_mine]
    residual = inputs + (keep + swap(send, "tp", n_tp, 1).astype(jnp.float32))

    scale_two = rms_scale(residual)
    mixed_low = (residual * scale_two * ffn_gain).astype(low)
    router_share = jax.nn.softmax(dot(mixed_low, w_router), axis=-1)
    gate = jnp.sum(router_share * choose_float, axis=-1)
    cotangent_sent = join(packed_cotangent, cotangent_first, cotangent_next)
    (cotangent_sent, expert_near), packed = ordered(
        (cotangent_sent, expert_near), pack(mixed_low)
    )
    first = first_wave(packed, "exp", n_exp, (4, 5, 1, 2))
    early = chosen(first, (4, 5, 1, 2))
    early, (packed, in_far) = ordered(early, (packed, in_far))
    first.update(early)
    then = next_wave(packed, "exp", n_exp, (6, 7, 3))
    if 3 in then:
        then[3], out_far = ordered(then[3], out_far)
    expert_all = [*expert_mine, *expert_near, in_far, out_far]
    expert_all += [swap(weights, "tp", n_tp, 1) for weights in (in_far, out_far)]
    received = join(packed, first, then).reshape(-1, width)

    produced_low, grad_sent, grad_rows, gate_grad_rows, active, grad_upper = expert_pass(
        received, cotangent_sent.reshape(-1, width), w_router, my_exp, expert_all
    )

    def thirds(value):
        first = value.astype(low)
        rest = value - first.astype(jnp.float32)
        second = rest.astype(low)
        third = (rest - second.astype(jnp.float32)).astype(low)
        return jnp.stack([first, second, third], axis=1)

    extra = thirds(gate_grad_rows.reshape(experts, capacity))
    extra = jnp.pad(extra, ((0, 0), (0, 0), (0, width // 3 - capacity))).reshape(experts, 1, width)
    grad_block = jnp.concatenate(
        [grad_sent.reshape(experts, capacity, width), extra], axis=1
    )
    first = first_wave(grad_block, "exp", n_exp, (4, 5, 1, 2, 3))
    pieces = (received, grad_upper, active, grad_rows)
    first[1], pieces = ordered(first[1], pieces)

    outer_send = expert_outer(*pieces, 1, low)
    early = chosen(first, (4, 1, 2, 3))
    (outer_send, early), (pieces, grad_block) = ordered((outer_send, early), (pieces, grad_block))
    first.update(early)
    then = next_wave(grad_block, "exp", n_exp, (6, 7))
    outer_given = swap(outer_send, "tp", n_tp, 1)
    outer_keep = expert_outer(*pieces, 0, low)
    outer_keep, (first, then) = ordered(outer_keep, (first, then))
    grad_block = join(grad_block, first, then)
    grad_back = unpack(grad_block[:, :capacity].reshape(-1, width))
    gate_parts = grad_block[:, capacity].reshape(experts, 3, width // 3)[:, :, :capacity]
    gate_flat = jnp.sum(gate_parts.astype(jnp.float32), axis=1).reshape(-1)
    gate_grad = jnp.sum(spread.astype(jnp.float32) * gate_flat[:, None], axis=0)

    upstream = cotangent.astype(jnp.float32)
    logit_grad = ((gate_grad * gate)[:, None] * (choose_float - router_share)).astype(low)
    grad_router = contract_first(mixed_low, logit_grad)
    grad_mixed = contract_last(logit_grad, w_router) + grad_back
    normal = residual * scale_two
    scaled = grad_mixed * ffn_gain
    grad_ffn_gain = jnp.sum(grad_mixed * normal, axis=0)
    grad_residual = upstream + scale_two * (
        scaled - normal * jnp.mean(scaled * normal, axis=-1, keepdims=True)
    )
    grad_low = grad_residual.astype(low)
    grad_other = swap(grad_low, "tp", n_tp, 1)

    outer_given, grad_other = ordered(outer_given, grad_other)

    def added(place, some):
        return outer_keep[place, some].astype(jnp.float32) + outer_given[place, some].astype(
            jnp.float32
        )

    across_in = swap(added(1, slice(0, width)).astype(low), "tp", n_tp, 2)
    grad_other, produced_low = ordered(grad_other, produced_low)
    produced_low = produced_low.reshape(experts, capacity, width)
    first = first_wave(produced_low, "exp", n_exp, (4, 5, 6, 7))

    grad_attn_far, folded_far, grad_normed = attend_back(
        core, kept_far, normed_low, normed_other, grad_low, grad_other, seqs, w_attn_far, base_far, None
    )
    (first, across_in, grad_attn_far), (folded_far, grad_normed, produced_low) = ordered(
        (first, across_in, grad_attn_far), (folded_far, grad_normed, produced_low)
    )
    then = next_wave(produced_low, "exp", n_exp, (1, 2, 3))
    grad_attn_far = swap(grad_attn_far, "tp", n_tp, 2)
    table_rows = bias_table.shape[0]
    table_far = swap(table_grad(folded_far, table_rows, length), "tp", n_tp, 2)
    grad_attn, folded, keep, send = attend_back(
        core, kept, normed_low, normed_other, grad_low, grad_other, seqs, w_attn, base, grad_normed
    )
    (then, grad_attn_far), (send, grad_attn) = ordered((then, grad_attn_far), (send, grad_attn))
    grad_normed = keep + swap(send, "tp", n_tp, 1).astype(jnp.float32)
    normal = inputs * scale_one
    scaled = grad_normed * attn_gain
    grad_attn_gain = jnp.sum(grad_normed * normal, axis=0)
    grad_tokens = grad_residual + scale_one * (
        scaled - normal * jnp.mean(scaled * normal, axis=-1, keepdims=True)
    )
    grad_table = table_grad(folded, table_rows, length) + table_far
    grad_attn = grad_attn + grad_attn_far.astype(jnp.float32)
    small = jnp.concatenate(
        [grad_attn_gain, grad_ffn_gain, grad_router.T.reshape(-1), grad_table.reshape(-1)]
    )
    small_size = (2 + experts) * width

    bits = [1 << place for place in range(n_exp.bit_length() - 1)]
    turned = bits[1:] + bits[:1]
    middle = grad_attn.shape[0] // 2
    wide = [grad_attn[:middle], grad_attn[middle:]]
    steps = [(halve, first_bit, second_bit) for first_bit, second_bit in zip(bits, turned)]
    steps += [(double, second, first_) for first_, second in zip(turned[::-1], bits[::-1])]
    small_steps = [None] + [("exp", n_exp, bit) for bit in bits]
    small_steps += [("tp", n_tp, 1 << place) for place in range(n_tp.bit_length() - 1)]
    small_steps += [None] * (len(steps) - len(small_steps))
    late = (first, then, outer_keep, outer_given)
    for place, (step, *both_bits) in enumerate(steps):
        if step is double and place == len(bits):
            wide = [value.astype(low) for value in wide]
        if place == len(steps) - 2:
            wide, (across_in, across_out) = ordered(wide, (across_in, across_out))
            across_out, wide = ordered(across_out, wide)
        wide = [step(value, "exp", n_exp, bit) for value, bit in zip(wide, both_bits)]
        if small_steps[place] is not None:
            axis, size, bit = small_steps[place]
            if axis == "tp" and bit == 1:
                grad_table = small[small_size:].reshape(grad_table.shape)
                small = small[:small_size]
            small = small + swap(small, axis, size, bit)
            wide, small = lax.optimization_barrier((wide, small))
        if place == 0:
            wide, late = ordered(wide, late)
            first, then, outer_keep, outer_given = late
            across_out = swap(added(1, slice(width, None)).astype(low), "tp", n_tp, 2)
            returned = unpack(join(produced_low, first, then).reshape(-1, width))
            mixed = (residual + gate[:, None] * returned).astype(low)
    grad_expert_in = (added(0, slice(0, width)) + across_in.astype(jnp.float32))[None]
    grad_expert_out = (added(0, slice(width, None)) + across_out.astype(jnp.float32))[None]
    grad_attn = jnp.concatenate(wide, axis=0).astype(jnp.float32)
    small = small.reshape(-1, width)
    return (
        mixed,
        grad_tokens,
        small[0],
        grad_attn[:head_width].T,
        grad_attn[head_width : 2 * head_width].T,
        grad_attn[2 * head_width : joint_width].T,
        grad_attn[joint_width:],
        grad_table,
        small[1],
        small[2:].T,
        grad_expert_in,
        grad_expert_out,
    )


def solution(mesh):
    placed = (
        P(("exp", "tp"), None),
        P("exp", None),
        P(("exp", "tp")),
        P(),
        P(None, "tp"),
        P(None, "tp"),
        P(None, "tp"),
        P("tp", None),
        P(None, "tp"),
        P(),
        P(),
        P("exp", None, "tp"),
        P("exp", "tp", None),
        P(("exp", "tp"), None),
    )
    return jax.shard_map(
        functools.partial(local, (mesh.shape["exp"], mesh.shape["tp"])),
        mesh=mesh,
        in_specs=placed,
        out_specs=(
            P(("exp", "tp"), None),
            P(("exp", "tp"), None),
            P(),
            P(None, "tp"),
            P(None, "tp"),
            P(None, "tp"),
            P("tp", None),
            P(None, "tp"),
            P(),
            P(),
            P("exp", None, "tp"),
            P("exp", "tp", None),
        ),
        check_vma=False,
    )
```

```python
import functools
import math

import jax
import jax.numpy as jnp
from jax import lax
from jax.experimental import pallas as pl
from jax.experimental.pallas import tpu as pltpu
from jax.sharding import PartitionSpec as P

HEAD_DIM = 64


EPSILON = 1e-06
MASKED_SCORE = -1000000000.0
thresholds = (8, 12, 16, 23, 32, 46, 64, 91)


def bucket_of(relative):
    distance = jnp.abs(relative)
    distant = 7 + sum(((distance >= boundary).astype(jnp.int32) for boundary in thresholds))
    return jnp.where(distance < 8, distance, distant) + jnp.where(relative > 0, 16, 0)


def bucket_onehot(relative, table_rows):
    return (
        bucket_of(relative)[..., None] == jnp.arange(table_rows, dtype=jnp.int32)
    ).astype(jnp.float32)


def rms_scale(values):
    return lax.rsqrt(jnp.mean(values * values, axis=-1, keepdims=True) + EPSILON)


def dot(left, right):
    return jnp.dot(left, right, preferred_element_type=jnp.float32)


def contract_first(left, right):
    return lax.dot_general(
        left, right, (((0,), (0,)), ((), ())), preferred_element_type=jnp.float32
    )


def contract_last(left, right):
    return lax.dot_general(
        left, right, (((1,), (1,)), ((), ())), preferred_element_type=jnp.float32
    )


def gelu_both(upper):
    slope = 0.7978845608028654
    cubic = slope * 0.044715
    square = upper * upper
    half = 0.5 + 0.5 * jnp.tanh(upper * (slope + cubic * square))
    active = upper * half
    derivative = half + active * (1.0 - half) * (2.0 * slope + 6.0 * cubic * square)
    return active, derivative


def swap(value, axis, size, bit):
    return lax.ppermute(value, axis, [(place, place ^ bit) for place in range(size)])


def trade_all(blocks, axis, size):
    stride = 1
    while stride < size:
        digit = min(8, size // stride)
        shape = blocks.shape
        view = blocks.reshape((size // (stride * digit), digit, stride) + shape[1:])
        parts = [view[:, 0]]
        for step in range(1, digit):
            parts.append(swap(view[:, step], axis, size, step * stride))
        blocks = jnp.stack(parts, axis=1).reshape(shape)
        stride *= digit
    return blocks


def first_wave(blocks, axis, size, steps):
    if size > 8:
        whole = trade_all(blocks, axis, size)
        return {step: whole[step] for step in range(1, size)}
    return {step: swap(blocks[step], axis, size, step) for step in steps if step < size}


def next_wave(blocks, axis, size, steps):
    if size > 8:
        return {}
    return {step: swap(blocks[step], axis, size, step) for step in steps if step < size}


def join(blocks, *waves):
    got = {0: blocks[0]}
    for wave in waves:
        got.update(wave)
    return jnp.stack([got[step] for step in range(blocks.shape[0])])


def chosen(wave, steps):
    return {step: wave[step] for step in steps if step in wave}


def ordered(earlier, later):
    return lax.optimization_barrier((earlier, later))


def halve(value, axis, size, bit):
    side = (lax.axis_index(axis) // bit) % 2
    half = value.shape[0] // 2
    keep = lax.dynamic_slice_in_dim(value, side * half, half, 0)
    send = lax.dynamic_slice_in_dim(value, (1 - side) * half, half, 0)
    return keep + swap(send.astype(jnp.bfloat16), axis, size, bit).astype(jnp.float32)


def double(value, axis, size, bit):
    other = swap(value, axis, size, bit)
    return jnp.where(
        (lax.axis_index(axis) // bit) % 2 == 0,
        jnp.concatenate([value, other], axis=0),
        jnp.concatenate([other, value], axis=0),
    )


def spread_diagonals(block, rows):
    held = block.shape[0]
    while held < rows:
        block = jnp.concatenate([block, pltpu.roll(block, held, 1)], axis=0)
        held *= 2
    return block


def fold_diagonals(block, rows):
    span = block.shape[1]
    while rows > 8:
        rows //= 2
        block = block[:rows] + pltpu.roll(block[rows:], span - rows, 1)
    return block


def masked_scores(key, query, bias, same):
    scores = contract_first(key, query) + bias
    return jnp.where(same, scores, MASKED_SCORE)


def expert_kernel(
    x_ref,
    g_ref,
    router_ref,
    mine_ref,
    *refs,
):
    weights = refs[:8]
    (
        produced_ref,
        sent_ref,
        grad_rows_ref,
        gate_ref,
        active_ref,
        upper_ref,
        held_ref,
        semaphores,
    ) = refs[8:]
    low = jnp.bfloat16
    width = x_ref.shape[1]
    first = pl.program_id(0) == 0
    copies = [
        pltpu.make_async_copy(weight, held_ref.at[place], semaphores.at[place])
        for place, weight in enumerate(weights)
    ]

    @pl.when(first)
    def _():
        for copy in copies:
            copy.start()

    logits = dot(x_ref[...], router_ref[...])
    logits = logits - jnp.max(logits, axis=1, keepdims=True)
    unscaled = jnp.exp(logits)
    gate = jnp.sum(unscaled * mine_ref[...], axis=1, keepdims=True) / jnp.sum(
        unscaled, axis=1, keepdims=True
    )
    grad_rows = (gate * g_ref[...].astype(jnp.float32)).astype(low)
    grad_rows_ref[...] = grad_rows
    produced = jnp.zeros(x_ref.shape, jnp.float32)
    sent = jnp.zeros(x_ref.shape, jnp.float32)
    for place in range(len(weights) // 2):

        @pl.when(first)
        def _():
            copies[2 * place].wait()
            copies[2 * place + 1].wait()

        weight_in = held_ref[2 * place]
        weight_out = held_ref[2 * place + 1]
        columns = pl.ds(place * width, width)
        active, derivative = gelu_both(dot(x_ref[...], weight_in))
        active = active.astype(low)
        upper = (contract_last(grad_rows, weight_out) * derivative).astype(low)
        active_ref[:, columns] = active
        upper_ref[:, columns] = upper
        produced = produced + dot(active, weight_out)
        sent = sent + contract_last(upper, weight_in)
    produced = produced.astype(low)
    produced_ref[...] = produced
    sent_ref[...] = sent.astype(low)
    gate_ref[...] = jnp.sum(
        g_ref[...].astype(jnp.float32) * produced.astype(jnp.float32), axis=1, keepdims=True
    )


def expert_pass(received, cotangent_rows, w_router, my_expert, weights):
    rows, width = received.shape
    experts = w_router.shape[1]
    tile = 240
    hidden = width * len(weights) // 2
    low = jnp.bfloat16
    is_mine = (jnp.arange(experts, dtype=jnp.int32) == my_expert).astype(jnp.float32)[None, :]
    tiled = lambda columns: pl.BlockSpec((tile, columns), lambda i: (i, 0))
    fixed = lambda *shape: pl.BlockSpec(shape, lambda i: (0,) * len(shape))
    shape = lambda columns, dtype: jax.ShapeDtypeStruct((rows, columns), dtype)
    return pl.pallas_call(
        expert_kernel,
        grid=(rows // tile,),
        in_specs=[tiled(width), tiled(width), fixed(width, experts), fixed(1, experts)]
        + [pl.BlockSpec(memory_space=pl.ANY)] * len(weights),
        out_specs=[
            tiled(width),
            tiled(width),
            tiled(width),
            tiled(1),
            tiled(hidden),
            tiled(hidden),
        ],
        out_shape=[
            shape(width, low),
            shape(width, low),
            shape(width, low),
            shape(1, jnp.float32),
            shape(hidden, low),
            shape(hidden, low),
        ],
        scratch_shapes=[
            pltpu.VMEM((len(weights), width, width), low),
            pltpu.SemaphoreType.DMA((len(weights),)),
        ],
        compiler_params=pltpu.CompilerParams(vmem_limit_bytes=48 * 1024 * 1024),
        cost_estimate=pl.CostEstimate(
            flops=rows * width * hidden * 8,
            bytes_accessed=rows * hidden * 4 + width * hidden * 4,
            transcendentals=rows * hidden,
        ),
        name="expert_pass",
    )(received, cotangent_rows, w_router, is_mine, *weights)


def outer_kernel(x_ref, upper_ref, active_ref, grad_ref, out_ref):
    width = x_ref.shape[1]
    out_ref[0, pl.ds(0, width)] = contract_first(x_ref[...], upper_ref[...]).astype(out_ref.dtype)
    out_ref[0, pl.ds(width, width)] = contract_first(active_ref[...], grad_ref[...]).astype(
        out_ref.dtype
    )


def expert_outer(received, grad_upper, active, grad_rows, first, dtype):
    rows, width = received.shape
    count = active.shape[1] // width // 2
    fixed = pl.BlockSpec((rows, width), lambda i: (0, 0))
    some = pl.BlockSpec((rows, width), lambda i: (0, 2 * i + first))
    return pl.pallas_call(
        outer_kernel,
        grid=(count,),
        in_specs=[fixed, some, some, fixed],
        out_specs=pl.BlockSpec((1, 2 * width, width), lambda i: (i, 0, 0)),
        out_shape=jax.ShapeDtypeStruct((count, 2 * width, width), dtype),
        compiler_params=pltpu.CompilerParams(vmem_limit_bytes=48 * 1024 * 1024),
        cost_estimate=pl.CostEstimate(
            flops=rows * width * width * 4 * count,
            bytes_accessed=rows * width * 8 + count * width * width * 8,
            transcendentals=0,
        ),
        name="expert_outer",
    )(received, grad_upper, active, grad_rows)


def sequence_rows(core_ref, pieces, per, held_ref):
    half = pieces[0].shape[0]
    for part in range(len(pieces) // 2):
        place = pl.program_id(0) * (len(pieces) // 2) + part
        is_mine = (place >= per) == (core_ref[0] == 1)

        @pl.when(is_mine)
        def _():
            held_ref[pl.ds(part * half, half)] = pieces[2 * part][...]

        @pl.when(jnp.logical_not(is_mine))
        def _():
            held_ref[pl.ds(part * half, half)] = pieces[2 * part + 1][...]


def part_rows(core_ref, value, per, keep_ref, send_ref):
    half = keep_ref.shape[0] // per
    count = value.shape[0] // half
    for part in range(count):
        place = pl.program_id(0) * count + part
        is_mine = (place >= per) == (core_ref[0] == 1)
        here = pl.ds(pl.multiple_of((place % per) * half, half), half)
        some = value[part * half : (part + 1) * half]

        @pl.when(is_mine)
        def _():
            keep_ref[here] = some

        @pl.when(jnp.logical_not(is_mine))
        def _():
            send_ref[here] = some.astype(send_ref.dtype)


def attend_kernel(heads, chunk, per, parts, last, core_ref, *refs):
    pieces, refs = refs[: 2 * parts], refs[2 * parts :]
    w_ref, base_ref, row_ref, column_ref, *refs = refs
    if last:
        given_ref, joint_ref, attended_ref, log_ref, keep_ref, send_ref, bias_ref, x_ref = refs
    else:
        joint_ref, attended_ref, log_ref, partial_ref, bias_ref, x_ref = refs
    low = jnp.bfloat16
    length = x_ref.shape[0]
    width = heads * HEAD_DIM

    @pl.when(pl.program_id(0) == 0)
    def _():
        for head in range(heads):
            bias_ref[head] = spread_diagonals(base_ref[head], length)[:, :length]

    sequence_rows(core_ref, pieces, per, x_ref)
    joint_ref[0] = contract_last(w_ref[pl.ds(0, 3 * width)], x_ref[...]).astype(low)
    work = [(head, start) for head in range(heads) for start in range(0, length, chunk)]

    def score(head, start):
        first = head * HEAD_DIM
        some = pl.ds(start, chunk)
        same = column_ref[0] == row_ref[0, :, some]
        key = joint_ref[0, pl.ds(width + first, HEAD_DIM)]
        query = joint_ref[0, pl.ds(first, HEAD_DIM), some]
        return masked_scores(key, query, bias_ref[head, :, some], same)

    ahead = score(*work[0])
    for place, (head, start) in enumerate(work):
        masked = ahead
        if place + 1 < len(work):
            ahead = score(*work[place + 1])
        first = head * HEAD_DIM
        some = pl.ds(start, chunk)
        peak = jnp.max(masked, axis=0, keepdims=True)
        unscaled = jnp.exp(masked - peak)
        total = jnp.sum(unscaled, axis=0, keepdims=True)
        weight_low = (unscaled * (1.0 / total)).astype(low)
        log_ref[0, pl.ds(head, 1), some] = peak + jnp.log(total)
        value = joint_ref[0, pl.ds(2 * width + first, HEAD_DIM)]
        attended_ref[0, pl.ds(first, HEAD_DIM), some] = dot(value, weight_low).astype(low)
    partial = contract_first(attended_ref[0], w_ref[pl.ds(3 * width, width)])
    if last:
        part_rows(core_ref, partial + given_ref[...], per, keep_ref, send_ref)
    else:
        partial_ref[...] = partial


def row_pieces(mine, other, length):
    rows, width = mine.shape
    half = math.gcd(rows, length)
    per = rows // half
    parts = length // half
    operands = []
    specs = []
    for part in range(parts):
        spec = pl.BlockSpec((half, width), lambda i, part=part: ((i * parts + part) % per, 0))
        operands += [mine, other]
        specs += [spec, spec]
    return operands, specs, per, parts


def attend(core, mine, other, segments, w_attn, base, given):
    seq_count, length = segments.shape
    rows, width = mine.shape
    total = seq_count * length
    joint_width = w_attn.shape[0] * 3 // 4
    head_width = joint_width // 3
    heads = head_width // HEAD_DIM
    chunk = min(length, 512)
    last = given is not None
    f32, low = jnp.float32, jnp.bfloat16
    fixed = lambda *shape: pl.BlockSpec(shape, lambda i: (0,) * len(shape))
    each = lambda *shape: pl.BlockSpec((1,) + shape, lambda i: (i, 0, 0))
    whole = pl.BlockSpec((length, width), lambda i: (i, 0))
    operands, specs, per, parts = row_pieces(mine, other, length)
    operands = [core] + operands + [w_attn, base, segments[:, None, :], segments[:, :, None]]
    specs = (
        [pl.BlockSpec(memory_space=pltpu.SMEM)]
        + specs
        + [
            fixed(joint_width + head_width, width),
            fixed(heads, 8, base.shape[2]),
            each(1, length),
            each(length, 1),
        ]
    )
    if last:
        operands.append(given)
        specs.append(whole)
        out_specs = [fixed(rows, width), fixed(rows, width)]
        out_shape = [
            jax.ShapeDtypeStruct((rows, width), f32),
            jax.ShapeDtypeStruct((rows, width), low),
        ]
    else:
        out_specs = [whole]
        out_shape = [jax.ShapeDtypeStruct((total, width), f32)]
    pairs = seq_count * heads * length * length
    return pl.pallas_call(
        functools.partial(attend_kernel, heads, chunk, per, parts, last),
        grid=(seq_count,),
        in_specs=specs,
        out_specs=[each(joint_width, length), each(head_width, length), each(8, length)]
        + out_specs,
        out_shape=[
            jax.ShapeDtypeStruct((seq_count, joint_width, length), low),
            jax.ShapeDtypeStruct((seq_count, head_width, length), low),
            jax.ShapeDtypeStruct((seq_count, 8, length), f32),
        ]
        + out_shape,
        scratch_shapes=[
            pltpu.VMEM((heads, length, length), f32),
            pltpu.VMEM((length, width), low),
        ],
        compiler_params=pltpu.CompilerParams(vmem_limit_bytes=28 * 1024 * 1024),
        cost_estimate=pl.CostEstimate(flops=1 << 20, bytes_accessed=1 << 16, transcendentals=0),
        name="attend",
    )(*operands)


def attend_back_kernel(heads, chunk, per, parts, last, core_ref, *refs):
    x_pieces, refs = refs[: 2 * parts], refs[2 * parts :]
    g_pieces, refs = refs[: 2 * parts], refs[2 * parts :]
    w_ref, base_ref, row_ref, column_ref, joint_ref, attended_ref, log_ref, *refs = refs
    if last:
        given_ref, w_grad_ref, table_ref, keep_ref, send_ref, *refs = refs
    else:
        w_grad_ref, table_ref, normed_ref, *refs = refs
    bias_ref, total_ref, back_ref, grad_ref, sum_ref, x_ref, g_ref = refs
    low = jnp.bfloat16
    length = x_ref.shape[0]
    width = heads * HEAD_DIM
    span = base_ref.shape[2]
    joint_rows = pl.ds(0, 3 * width)
    out_rows = pl.ds(3 * width, width)

    @pl.when(pl.program_id(0) == 0)
    def _():
        for head in range(heads):
            bias_ref[head] = spread_diagonals(base_ref[head], length)[:, :length]
        total_ref[...] = jnp.zeros_like(total_ref)
        sum_ref[...] = jnp.zeros_like(sum_ref)

    sequence_rows(core_ref, x_pieces, per, x_ref)
    sequence_rows(core_ref, g_pieces, per, g_ref)
    sum_ref[out_rows] += dot(attended_ref[0], g_ref[...])
    back_ref[...] = contract_last(w_ref[out_rows], g_ref[...]).astype(low)
    for head in range(heads):
        first = head * HEAD_DIM
        here = pl.ds(first, HEAD_DIM)
        key = joint_ref[0, pl.ds(width + first, HEAD_DIM)]
        value = joint_ref[0, pl.ds(2 * width + first, HEAD_DIM)]
        grad_key = 0.0
        grad_value = 0.0
        for start in range(0, length, chunk):
            some = pl.ds(start, chunk)
            query = joint_ref[0, here, some]
            back = back_ref[here, some]
            same = column_ref[0] == row_ref[0, :, some]
            masked = masked_scores(key, query, bias_ref[head, :, some], same)
            weight = jnp.exp(masked - log_ref[0, pl.ds(head, 1), some])
            grad_weight = contract_first(value, back)
            grad_value = grad_value + contract_last(back, weight.astype(low))
            delta = jnp.sum(weight * grad_weight, axis=0, keepdims=True)
            grad_scores = (weight * (grad_weight - delta)).astype(low)
            total_ref[head, :, some] += grad_scores.astype(jnp.float32)
            grad_key = grad_key + contract_last(query, grad_scores)
            grad_ref[here, some] = dot(key, grad_scores).astype(low)
        grad_ref[pl.ds(width + first, HEAD_DIM), :] = grad_key.astype(low)
        grad_ref[pl.ds(2 * width + first, HEAD_DIM), :] = grad_value.astype(low)
    sum_ref[joint_rows] += dot(grad_ref[...], x_ref[...])
    normed = contract_first(grad_ref[...], w_ref[joint_rows])
    if last:
        part_rows(core_ref, normed + given_ref[...], per, keep_ref, send_ref)
    else:
        normed_ref[...] = normed

    @pl.when(pl.program_id(0) == pl.num_programs(0) - 1)
    def _():
        w_grad_ref[...] = sum_ref[...].astype(w_grad_ref.dtype)
        for head in range(heads):
            padded = jnp.concatenate(
                [total_ref[head], jnp.zeros((length, span - length), jnp.float32)], axis=1
            )
            table_ref[head] = fold_diagonals(padded, length)


def attend_back(core, kept, mine, other, grad_mine, grad_other, segments, w_attn, base, given):
    joint, attended, logs = kept
    seq_count, length = segments.shape
    rows, width = mine.shape
    total = seq_count * length
    attn_rows = w_attn.shape[0]
    joint_width = attn_rows * 3 // 4
    head_width = joint_width // 3
    heads = head_width // HEAD_DIM
    chunk = min(length, 512)
    last = given is not None
    f32, low = jnp.float32, jnp.bfloat16
    fixed = lambda *shape: pl.BlockSpec(shape, lambda i: (0,) * len(shape))
    each = lambda *shape: pl.BlockSpec((1,) + shape, lambda i: (i, 0, 0))
    whole = pl.BlockSpec((length, width), lambda i: (i, 0))
    operands, specs, per, parts = row_pieces(mine, other, length)
    grad_operands, grad_specs, _, _ = row_pieces(grad_mine, grad_other, length)
    operands = (
        [core]
        + operands
        + grad_operands
        + [w_attn, base, segments[:, None, :], segments[:, :, None], joint, attended, logs]
    )
    specs = (
        [pl.BlockSpec(memory_space=pltpu.SMEM)]
        + specs
        + grad_specs
        + [
            fixed(attn_rows, width),
            fixed(heads, 8, base.shape[2]),
            each(1, length),
            each(length, 1),
            each(joint_width, length),
            each(head_width, length),
            each(8, length),
        ]
    )
    if last:
        operands.append(given)
        specs.append(whole)
        out_specs = [fixed(rows, width), fixed(rows, width)]
        out_shape = [
            jax.ShapeDtypeStruct((rows, width), f32),
            jax.ShapeDtypeStruct((rows, width), low),
        ]
    else:
        out_specs = [whole]
        out_shape = [jax.ShapeDtypeStruct((total, width), f32)]
    pairs = seq_count * heads * length * length
    return pl.pallas_call(
        functools.partial(attend_back_kernel, heads, chunk, per, parts, last),
        grid=(seq_count,),
        in_specs=specs,
        out_specs=[fixed(attn_rows, width), fixed(heads, 8, base.shape[2])] + out_specs,
        out_shape=[
            jax.ShapeDtypeStruct((attn_rows, width), f32 if last else low),
            jax.ShapeDtypeStruct((heads, 8, base.shape[2]), f32),
        ]
        + out_shape,
        scratch_shapes=[
            pltpu.VMEM((heads, length, length), f32),
            pltpu.VMEM((heads, length, length), f32),
            pltpu.VMEM((head_width, length), low),
            pltpu.VMEM((joint_width, length), low),
            pltpu.VMEM((attn_rows, width), f32),
            pltpu.VMEM((length, width), low),
            pltpu.VMEM((length, width), low),
        ],
        compiler_params=pltpu.CompilerParams(vmem_limit_bytes=32 * 1024 * 1024),
        cost_estimate=pl.CostEstimate(
            flops=pairs * HEAD_DIM * 40 + total * width * head_width * 16,
            bytes_accessed=total * width * 16 + joint_width * width * 8,
            transcendentals=pairs,
        ),
        name="attend_back",
    )(*operands)


def bias_base(table, length):
    span = 2 * length
    offset = jnp.arange(span, dtype=jnp.int32)[None, :] - jnp.arange(8, dtype=jnp.int32)[:, None]
    offset = jnp.where(offset < 0, offset + span, offset)
    relative = jnp.where(offset < length, -offset, span - offset)
    onehot = bucket_onehot(relative, table.shape[0])
    return jnp.einsum("stb,bh->hst", onehot, table, precision=lax.Precision.HIGHEST)


def table_grad(folded, table_rows, length):
    span = 2 * length
    offset = jnp.arange(span, dtype=jnp.int32)[None, :] - jnp.arange(8, dtype=jnp.int32)[:, None]
    offset = jnp.where(offset < 0, offset + span, offset)
    relative = jnp.where(offset < length, -offset, span - offset)
    onehot = bucket_onehot(relative, table_rows)
    return jnp.einsum("stb,hst->bh", onehot, folded, precision=lax.Precision.HIGHEST)


def local(
    sizes,
    tokens,
    segments,
    routes,
    attn_gain,
    w_query,
    w_key,
    w_value,
    w_output,
    bias_table,
    ffn_gain,
    w_router,
    expert_in,
    expert_out,
    cotangent,
):
    n_exp, n_tp = sizes
    rows, width = tokens.shape
    group_seqs, length = segments.shape
    head_width = w_query.shape[1]
    experts = w_router.shape[1]
    capacity = rows * 5 // (4 * experts)
    low = jnp.bfloat16
    my_exp = lax.axis_index("exp")
    my_tp = lax.axis_index("tp")
    my_core = my_tp % 2
    pair_seqs = group_seqs * 2 // n_tp
    seqs = lax.dynamic_slice_in_dim(segments, (my_tp // 2) * pair_seqs, pair_seqs, 0)

    core = my_core.astype(jnp.int32)[None]

    joint_width = 3 * head_width
    w_attn = jnp.concatenate([w_query.T, w_key.T, w_value.T, w_output], axis=0)
    table_far = swap(bias_table, "tp", n_tp, 2)
    table_far, w_attn = ordered(table_far, w_attn)
    w_attn_far = swap(w_attn, "tp", n_tp, 2)
    expert_mine = [expert_in[0], expert_out[0]]
    w_attn_far, out_mine = ordered(w_attn_far, expert_mine[1])
    out_far = swap(out_mine, "tp", n_tp, 2)

    place = jnp.arange(rows, dtype=jnp.int32)
    choose = routes[:, None] == jnp.arange(experts, dtype=jnp.int32)[None, :]
    choose_float = choose.astype(jnp.float32)
    rank = dot((place[:, None] > place[None, :]).astype(low), choose.astype(low))
    slot = jnp.sum(rank * choose_float, axis=-1).astype(jnp.int32)
    target = jnp.where(slot < capacity, (routes ^ my_exp) * capacity + slot, experts * capacity)
    spread = (
        target[None, :] == jnp.arange(experts * capacity, dtype=jnp.int32)[:, None]
    ).astype(low)

    def pack(data):
        return dot(spread, data).astype(low).reshape(experts, capacity, width)

    def unpack(data):
        return contract_first(spread, data)

    packed_cotangent = pack(cotangent)
    cotangent_first = first_wave(packed_cotangent, "exp", n_exp, (4, 5, 1))

    inputs = tokens.astype(jnp.float32)
    scale_one = rms_scale(inputs)
    normed_low = (inputs * scale_one * attn_gain).astype(low)
    normed_other = swap(normed_low, "tp", n_tp, 1)
    normed_other, expert_mine = ordered(normed_other, expert_mine)
    in_far = swap(expert_mine[0], "tp", n_tp, 2)
    base = bias_base(bias_table, length)
    *kept, partial = attend(core, normed_low, normed_other, seqs, w_attn, base, None)
    partial, (packed_cotangent, table_far) = ordered(partial, (packed_cotangent, table_far))
    base_far = bias_base(table_far, length)
    cotangent_first, partial = ordered(cotangent_first, partial)
    cotangent_next = next_wave(packed_cotangent, "exp", n_exp, (6, 7, 2, 3))


    *kept_far, keep, send = attend(
        core, normed_low, normed_other, seqs, w_attn_far, base_far, partial
    )
    cotangent_next, (send, expert_mine) = ordered(cotangent_next, (send, expert_mine))
    expert_near = [swap(weights, "tp", n_tp, 1) for weights in expert_mine]
    residual = inputs + (keep + swap(send, "tp", n_tp, 1).astype(jnp.float32))

    scale_two = rms_scale(residual)
    mixed_low = (residual * scale_two * ffn_gain).astype(low)
    router_share = jax.nn.softmax(dot(mixed_low, w_router), axis=-1)
    gate = jnp.sum(router_share * choose_float, axis=-1)
    cotangent_sent = join(packed_cotangent, cotangent_first, cotangent_next)
    (cotangent_sent, expert_near), packed = ordered(
        (cotangent_sent, expert_near), pack(mixed_low)
    )
    first = first_wave(packed, "exp", n_exp, (4, 5, 1, 2))
    early = chosen(first, (4, 5, 1, 2))
    early, (packed, in_far) = ordered(early, (packed, in_far))
    first.update(early)
    then = next_wave(packed, "exp", n_exp, (6, 7, 3))
    if 3 in then:
        then[3], out_far = ordered(then[3], out_far)
    expert_all = [*expert_mine, *expert_near, in_far, out_far]
    expert_all += [swap(weights, "tp", n_tp, 1) for weights in (in_far, out_far)]
    received = join(packed, first, then).reshape(-1, width)

    produced_low, grad_sent, grad_rows, gate_grad_rows, active, grad_upper = expert_pass(
        received, cotangent_sent.reshape(-1, width), w_router, my_exp, expert_all
    )

    def thirds(value):
        first = value.astype(low)
        rest = value - first.astype(jnp.float32)
        second = rest.astype(low)
        third = (rest - second.astype(jnp.float32)).astype(low)
        return jnp.stack([first, second, third], axis=1)

    extra = thirds(gate_grad_rows.reshape(experts, capacity))
    extra = jnp.pad(extra, ((0, 0), (0, 0), (0, width // 3 - capacity))).reshape(experts, 1, width)
    grad_block = jnp.concatenate(
        [grad_sent.reshape(experts, capacity, width), extra], axis=1
    )
    first = first_wave(grad_block, "exp", n_exp, (4, 5, 1, 2, 3))
    pieces = (received, grad_upper, active, grad_rows)
    first[1], pieces = ordered(first[1], pieces)

    outer_send = expert_outer(*pieces, 1, low)
    early = chosen(first, (4, 1, 2, 3))
    (outer_send, early), (pieces, grad_block) = ordered((outer_send, early), (pieces, grad_block))
    first.update(early)
    then = next_wave(grad_block, "exp", n_exp, (6, 7))
    outer_given = swap(outer_send, "tp", n_tp, 1)
    outer_keep = expert_outer(*pieces, 0, low)
    outer_keep, (first, then) = ordered(outer_keep, (first, then))
    grad_block = join(grad_block, first, then)
    grad_back = unpack(grad_block[:, :capacity].reshape(-1, width))
    gate_parts = grad_block[:, capacity].reshape(experts, 3, width // 3)[:, :, :capacity]
    gate_flat = jnp.sum(gate_parts.astype(jnp.float32), axis=1).reshape(-1)
    gate_grad = jnp.sum(spread.astype(jnp.float32) * gate_flat[:, None], axis=0)

    upstream = cotangent.astype(jnp.float32)
    logit_grad = ((gate_grad * gate)[:, None] * (choose_float - router_share)).astype(low)
    grad_router = contract_first(mixed_low, logit_grad)
    grad_mixed = contract_last(logit_grad, w_router) + grad_back
    normal = residual * scale_two
    scaled = grad_mixed * ffn_gain
    grad_ffn_gain = jnp.sum(grad_mixed * normal, axis=0)
    grad_residual = upstream + scale_two * (
        scaled - normal * jnp.mean(scaled * normal, axis=-1, keepdims=True)
    )
    grad_low = grad_residual.astype(low)
    grad_other = swap(grad_low, "tp", n_tp, 1)

    outer_given, grad_other = ordered(outer_given, grad_other)

    def added(place, some):
        return outer_keep[place, some].astype(jnp.float32) + outer_given[place, some].astype(
            jnp.float32
        )

    across_in = swap(added(1, slice(0, width)).astype(low), "tp", n_tp, 2)
    grad_other, produced_low = ordered(grad_other, produced_low)
    produced_low = produced_low.reshape(experts, capacity, width)
    first = first_wave(produced_low, "exp", n_exp, (4, 5, 6, 7))

    grad_attn_far, folded_far, grad_normed = attend_back(
        core, kept_far, normed_low, normed_other, grad_low, grad_other, seqs, w_attn_far, base_far, None
    )
    (first, across_in, grad_attn_far), (folded_far, grad_normed, produced_low) = ordered(
        (first, across_in, grad_attn_far), (folded_far, grad_normed, produced_low)
    )
    then = next_wave(produced_low, "exp", n_exp, (1, 2, 3))
    grad_attn_far = swap(grad_attn_far, "tp", n_tp, 2)
    table_rows = bias_table.shape[0]
    table_far = swap(table_grad(folded_far, table_rows, length), "tp", n_tp, 2)
    grad_attn, folded, keep, send = attend_back(
        core, kept, normed_low, normed_other, grad_low, grad_other, seqs, w_attn, base, grad_normed
    )
    (then, grad_attn_far), (send, grad_attn) = ordered((then, grad_attn_far), (send, grad_attn))
    grad_normed = keep + swap(send, "tp", n_tp, 1).astype(jnp.float32)
    normal = inputs * scale_one
    scaled = grad_normed * attn_gain
    grad_attn_gain = jnp.sum(grad_normed * normal, axis=0)
    grad_tokens = grad_residual + scale_one * (
        scaled - normal * jnp.mean(scaled * normal, axis=-1, keepdims=True)
    )
    grad_table = table_grad(folded, table_rows, length) + table_far
    grad_attn = grad_attn + grad_attn_far.astype(jnp.float32)
    small = jnp.concatenate(
        [grad_attn_gain, grad_ffn_gain, grad_router.T.reshape(-1), grad_table.reshape(-1)]
    )
    small_size = (2 + experts) * width

    bits = [1 << place for place in range(n_exp.bit_length() - 1)]
    turned = bits[1:] + bits[:1]
    middle = grad_attn.shape[0] // 2
    wide = [grad_attn[:middle], grad_attn[middle:]]
    steps = [(halve, first_bit, second_bit) for first_bit, second_bit in zip(bits, turned)]
    steps += [(double, second, first_) for first_, second in zip(turned[::-1], bits[::-1])]
    small_steps = [None] + [("exp", n_exp, bit) for bit in bits]
    small_steps += [("tp", n_tp, 1 << place) for place in range(n_tp.bit_length() - 1)]
    small_steps += [None] * (len(steps) - len(small_steps))
    late = (first, then, outer_keep, outer_given)
    for place, (step, *both_bits) in enumerate(steps):
        if step is double and place == len(bits):
            wide = [value.astype(low) for value in wide]
        if place == len(steps) - 2:
            wide, (across_in, across_out) = ordered(wide, (across_in, across_out))
            across_out, wide = ordered(across_out, wide)
        wide = [step(value, "exp", n_exp, bit) for value, bit in zip(wide, both_bits)]
        if small_steps[place] is not None:
            axis, size, bit = small_steps[place]
            if axis == "tp" and bit == 1:
                grad_table = small[small_size:].reshape(grad_table.shape)
                small = small[:small_size]
            small = small + swap(small, axis, size, bit)
            wide, small = lax.optimization_barrier((wide, small))
        if place == 0:
            wide, late = ordered(wide, late)
            first, then, outer_keep, outer_given = late
            across_out = swap(added(1, slice(width, None)).astype(low), "tp", n_tp, 2)
            returned = unpack(join(produced_low, first, then).reshape(-1, width))
            mixed = (residual + gate[:, None] * returned).astype(low)
    grad_expert_in = (added(0, slice(0, width)) + across_in.astype(jnp.float32))[None]
    grad_expert_out = (added(0, slice(width, None)) + across_out.astype(jnp.float32))[None]
    grad_attn = jnp.concatenate(wide, axis=0).astype(jnp.float32)
    small = small.reshape(-1, width)
    return (
        mixed,
        grad_tokens,
        small[0],
        grad_attn[:head_width].T,
        grad_attn[head_width : 2 * head_width].T,
        grad_attn[2 * head_width : joint_width].T,
        grad_attn[joint_width:],
        grad_table,
        small[1],
        small[2:].T,
        grad_expert_in,
        grad_expert_out,
    )


def solution(mesh):
    placed = (
        P(("exp", "tp"), None),
        P("exp", None),
        P(("exp", "tp")),
        P(),
        P(None, "tp"),
        P(None, "tp"),
        P(None, "tp"),
        P("tp", None),
        P(None, "tp"),
        P(),
        P(),
        P("exp", None, "tp"),
        P("exp", "tp", None),
        P(("exp", "tp"), None),
    )
    return jax.shard_map(
        functools.partial(local, (mesh.shape["exp"], mesh.shape["tp"])),
        mesh=mesh,
        in_specs=placed,
        out_specs=(
            P(("exp", "tp"), None),
            P(("exp", "tp"), None),
            P(),
            P(None, "tp"),
            P(None, "tp"),
            P(None, "tp"),
            P("tp", None),
            P(None, "tp"),
            P(),
            P(),
            P("exp", None, "tp"),
            P("exp", "tp", None),
        ),
        check_vma=False,
    )
```
